256 devices in a mesh: sx: 32 (over x, y, z_lo), sy: 8 (over z_hi, core).
Axes of the slice: x: 4, y: 4, z: 8 (z_hi: 4, z_lo: 2; z = z_hi * 2 + z_lo), core: 2. Of those that a mesh axis runs over, the one named last changes fastest.
Arguments:
- weights_in: float32 [2, 32, 32, 8, 4096], P(None, None, 'sx', 'sy'), may hold values from -2.5 to 2.5
- speed_modes: float32 [4, 4], replicated, may hold values from -0.04 to 0.04
Outputs:
- weights_out: float32 [2, 32, 32, 8, 4096], P(None, None, 'sx', 'sy')
The draws below stay inside these ranges and needn't reach their ends.
All inputs are finite; a program needn't handle non-finite values.
Results may differ from the reference program's by a relative error of at most 0.0007.
Values sent between devices are 32-bit elements; how exact they have to be, the bound alone decides.
A program may use at most 128 MiB of HBM per device.

```python
import math
import jax
import jax.numpy as jnp
import numpy as np
from jax import lax

GRID = 8192
CHEB0 = 4
CHEB1 = 8
RANK = 32
SPAT = 8
FREQ0 = 4
FREQ1 = 16
MODES = 4
PAIRS = 4096
N_SX = 32
N_SY = 8


def level_of(own_key, extent, split, low, high):
    level = 1.0
    for axis_at, shards_of in split:
        steps = jax.random.uniform(jax.random.fold_in(jax.random.fold_in(own_key, 6), axis_at), (shards_of,), jnp.float32, low / len(split), high / len(split))
        level = level * jnp.repeat(jnp.exp(steps), extent[axis_at] // shards_of).reshape((-1,) + (1,) * (len(extent) - 1 - axis_at))
    return level


def noise(own_key, extent, scale, reach, split=(), held_as=jnp.bfloat16):
    loudness = level_of(own_key, extent, split, -0.22, 0.18) if split else 1.0
    result = jax.random.normal(own_key, extent, jnp.float32) * scale * loudness
    return jnp.minimum(jnp.maximum(result, -reach), reach).astype(held_as)


def setup_inputs(seed: int = 0) -> dict:
    key_list = jax.random.split(jax.random.key(seed), 3)
    weights_in = noise(key_list[0], (2, RANK, N_SX, N_SY, PAIRS), 0.25, 2.5, ((2, 32), (3, 8)), jnp.float32)
    speed_modes = jnp.clip(jax.random.uniform(key_list[1], (MODES, MODES), jnp.float32, -0.04, 0.04), -0.04, 0.04)
    return dict(weights_in=weights_in, speed_modes=speed_modes)


def cheb_nodes(node_count):
    return np.cos((2.0 * np.arange(node_count) + 1.0) * np.pi / (2.0 * node_count))

def child_table(node_count, child_bit):
    node_values = cheb_nodes(node_count)
    child_points = child_bit - 0.5 + 0.5 * node_values
    lagrange = np.ones((node_count, node_count))
    for k in range(node_count):
        for j in range(node_count):
            if j != k:
                lagrange[k, :] = lagrange[k, :] * (child_points - node_values[j]) / (node_values[k] - node_values[j])
    return lagrange

def merge_matrix(split_dim, child_bit):
    if split_dim == 0:
        combined = np.kron(child_table(CHEB0, child_bit), np.eye(CHEB1))
    else:
        combined = np.kron(np.eye(CHEB0), child_table(CHEB1, child_bit))
    return jnp.asarray(combined, dtype=jnp.float32)

def node_grids():
    grid_x = jnp.asarray(np.repeat(cheb_nodes(CHEB0), CHEB1), dtype=jnp.float32)
    grid_y = jnp.asarray(np.tile(cheb_nodes(CHEB1), CHEB0), dtype=jnp.float32)
    return (grid_x, grid_y)

def reverse_bits(position, bit_count):
    result_bits = position * 0
    for t in range(bit_count):
        result_bits = result_bits + position // 2 ** t % 2 * 2 ** (bit_count - 1 - t)
    return result_bits

def level_order(levels_x, levels_y):
    order_list = []
    done_x = 0
    done_y = 0
    while done_x < levels_x or done_y < levels_y:
        if done_x < levels_x and (done_x <= done_y or done_y >= levels_y):
            order_list.append((0, done_x, done_y))
            done_x = done_x + 1
        else:
            order_list.append((1, done_x, done_y))
            done_y = done_y + 1
    return order_list

def dim_geometry(device_coord, start_box, high_box, count_dev, high_count, done_count, merged, flipped):
    box_width = GRID / (high_count * count_dev) * 2 ** done_count
    spatial = start_box * 2 ** done_count + reverse_bits(device_coord, done_count)
    if merged:
        parity = device_coord // 2 ** done_count % 2
        side_bit = 1 - parity if flipped else parity
        spatial = spatial * 2 + side_bit
        cell_width = 1.0 / (SPAT * 2 ** (done_count + 1))
        parent = high_box * (count_dev // 2 ** (done_count + 1)) + device_coord // 2 ** (done_count + 1)
        middle = -0.5 * GRID + (parent.astype(jnp.float32) + 0.5) * (2.0 * box_width)
        half_width = box_width
    else:
        parity = None
        cell_width = 1.0 / (SPAT * 2 ** done_count)
        parent = high_box * (count_dev // 2 ** done_count) + device_coord // 2 ** done_count
        middle = -0.5 * GRID + (parent.astype(jnp.float32) + 0.5) * box_width
        half_width = 0.5 * box_width
    position = -0.5 + (spatial.astype(jnp.float32) + 0.5) * cell_width
    return (position, middle, half_width, parity)

def speed_at(speed_modes, position_x, position_y):
    summed = 0.3 + 0.0 * (position_x + position_y)
    waves_x = [jnp.cos(math.pi * j * (position_x + 0.5)) for j in range(MODES)]
    waves_y = [jnp.cos(math.pi * k * (position_y + 0.5)) for k in range(MODES)]
    for j in range(MODES):
        for k in range(MODES):
            summed = summed + speed_modes[j, k] * waves_x[j] * waves_y[k]
    return summed

def spread_rank(vector, rank_dims):
    return vector.reshape((vector.shape[0],) + (1,) * rank_dims)

def phase_angle(shift_x, shift_y, geo_x, geo_y, speed_here):
    position_x, middle_x = (geo_x[0], geo_x[1])
    position_y, middle_y = (geo_y[0], geo_y[1])
    quadratic = shift_x * (shift_x + 2.0 * middle_x) + shift_y * (shift_y + 2.0 * middle_y)
    root_here = jnp.sqrt(1.0 + (middle_x + shift_x) ** 2 + (middle_y + shift_y) ** 2)
    root_middle = jnp.sqrt(1.0 + middle_x ** 2 + middle_y ** 2)
    phase_turn = position_x * shift_x + position_y * shift_y + speed_here * quadratic / (root_here + root_middle)
    return 2.0 * math.pi * phase_turn

def rotate(pair_array, phase_turn, turn_sign):
    cos_part = jnp.cos(phase_turn)
    sin_part = turn_sign * jnp.sin(phase_turn)
    return jnp.stack([cos_part * pair_array[0] - sin_part * pair_array[1], sin_part * pair_array[0] + cos_part * pair_array[1]])

def child_shifts(split_dim, offset, geo_x, geo_y):
    grid_x, grid_y = node_grids()
    half_x, half_y = (geo_x[2], geo_y[2])
    if offset is None:
        return (half_x * grid_x, half_y * grid_y)
    if split_dim == 0:
        return (half_x * (offset - 0.5 + 0.5 * grid_x), half_y * grid_y)
    return (half_x * grid_x, half_y * (offset - 0.5 + 0.5 * grid_y))

def translate(source, offset, matrix, split_dim, geo_x, geo_y, speed_here):
    rank_dims = source.ndim - 2
    shift_x, shift_y = child_shifts(split_dim, offset, geo_x, geo_y)
    phase_turn = phase_angle(spread_rank(shift_x, rank_dims), spread_rank(shift_y, rank_dims), geo_x, geo_y, speed_here)
    turned = rotate(source, phase_turn, 1.0)
    return jnp.einsum('ts,ks...->kt...', matrix, turned, precision=lax.Precision.HIGHEST)

def finish(summed, split_dim, geo_x, geo_y, speed_here):
    rank_dims = summed.ndim - 2
    shift_x, shift_y = child_shifts(split_dim, None, geo_x, geo_y)
    phase_turn = phase_angle(spread_rank(shift_x, rank_dims), spread_rank(shift_y, rank_dims), geo_x, geo_y, speed_here)
    return rotate(summed, phase_turn, -1.0)

def level_update(current, partner, parity, split_dim, geo_x, geo_y, speed_modes):
    speed_here = speed_at(speed_modes, geo_x[0], geo_y[0])
    first_term = translate(jnp.where(parity == 0, current, partner), 0, merge_matrix(split_dim, 0), split_dim, geo_x, geo_y, speed_here)
    second_term = translate(jnp.where(parity == 0, partner, current), 1, merge_matrix(split_dim, 1), split_dim, geo_x, geo_y, speed_here)
    return finish(first_term + second_term, split_dim, geo_x, geo_y, speed_here)

def flip_partner(current, axis_pos, done_count, axis_count):
    shape_now = current.shape
    split_shape = shape_now[:axis_pos] + (axis_count // 2 ** (done_count + 1), 2, 2 ** done_count) + shape_now[axis_pos + 1:]
    return jnp.flip(current.reshape(split_shape), axis_pos + 1).reshape(shape_now)

def reference(weights_in, speed_modes):
    coord_x = jnp.arange(N_SX, dtype=jnp.int32).reshape(N_SX, 1, 1)
    coord_y = jnp.arange(N_SY, dtype=jnp.int32).reshape(1, N_SY, 1)
    pair_index = jnp.arange(PAIRS, dtype=jnp.int32).reshape(1, 1, PAIRS)
    high_y = pair_index % FREQ1
    high_x = pair_index // FREQ1 % FREQ0
    start_y = pair_index // (FREQ1 * FREQ0) % SPAT
    start_x = pair_index // (FREQ1 * FREQ0 * SPAT)
    current = weights_in
    for split_dim, done_x, done_y in level_order(N_SX.bit_length() - 1, N_SY.bit_length() - 1):
        geo_x = dim_geometry(coord_x, start_x, high_x, N_SX, FREQ0, done_x, split_dim == 0, False)
        geo_y = dim_geometry(coord_y, start_y, high_y, N_SY, FREQ1, done_y, split_dim == 1, False)
        if split_dim == 0:
            partner = flip_partner(current, 2, done_x, N_SX)
            parity = geo_x[3]
        else:
            partner = flip_partner(current, 3, done_y, N_SY)
            parity = geo_y[3]
        current = level_update(current, partner, parity, split_dim, geo_x, geo_y, speed_modes)
    return current
```

```python
import functools

import jax
import jax.numpy as jnp
import numpy as np
from jax import lax
from jax.experimental import pallas as pl
from jax.experimental.pallas import tpu as pltpu
from jax.sharding import PartitionSpec as P

MESH = pl.DeviceIdType.MESH
GRID = 8192
CHEB = (4, 8)
SPAT = 8
FREQ = (4, 16)
COUNT = (32, 8)
MODES = 4
TILE = (8, 128)
LEVELS = ((0, 0, 0), (1, 1, 0), (0, 1, 1), (1, 2, 1), (0, 2, 2), (1, 3, 2), (0, 3, 3), (0, 4, 3))
SIN_POLY = (4.44288292, -7.30824569, 3.60635422, -0.84611165, 0.10982452)
COS_POLY = (1.4142135, -6.97885095, 5.73946038, -1.88355791, 0.31068803)


def cheb_nodes(q):
    return np.cos((2.0 * np.arange(q) + 1.0) * np.pi / (2.0 * q))


NODES = tuple(np.asarray(cheb_nodes(q), np.float32).astype(np.float64) for q in CHEB)


def child_table(q):
    z = cheb_nodes(q)
    points = -0.5 + 0.5 * z
    table = np.ones((q, q))
    for k in range(q):
        for j in range(q):
            if j != k:
                table[k, :] *= (points - z[j]) / (z[k] - z[j])
    return table


def halves(q):
    table = child_table(q)
    even = 0.5 * (table + table[::-1])[: q // 2]
    odd = 0.5 * (table - table[::-1])[: q // 2]
    return even, odd


HALVES = tuple(halves(q) for q in CHEB)


def merge(q, a, b):
    even, odd = HALVES[0 if q == 4 else 1]
    plus = [a[k] + b[q - 1 - k] for k in range(q)]
    minus = [a[k] - b[q - 1 - k] for k in range(q)]
    out = [None] * q
    for k in range(q // 2):
        e = plus[0] * float(even[k, 0])
        o = minus[0] * float(odd[k, 0])
        for j in range(1, q):
            e = e + plus[j] * float(even[k, j])
            o = o + minus[j] * float(odd[k, j])
        out[k] = e + o
        out[q - 1 - k] = e - o
    return out


def frac(v):
    return v - jnp.round(v)


def poly(coefficients, t):
    result = t * coefficients[-1] + coefficients[-2]
    for value in coefficients[-3::-1]:
        result = result * t + value
    return result


def turn(angle):
    r = frac(angle)
    t = r * r
    s = poly(SIN_POLY, t) * r
    c = poly(COS_POLY, t)
    return 1.0 - s * s, s * c


def node(e, k):
    value = jnp.float32(NODES[e][0])
    for i in range(1, CHEB[e]):
        value = jnp.where(k == i, jnp.float32(NODES[e][i]), value)
    return value


def rev(v, bits):
    result = jnp.int32(0)
    for t in range(bits):
        result = result + ((v >> t) & 1) * (1 << (bits - 1 - t))
    return result


def place(start, coord, done):
    index = start * (1 << done) + rev(coord, done)
    return (index.astype(jnp.float32) + 0.5) * (1.0 / (SPAT << done)) - 0.5


def width(e, done):
    return float(GRID // (FREQ[e] * COUNT[e]) * (1 << done))


def middle(e, high, coord, done):
    index = high * (COUNT[e] >> done) + (coord >> done)
    return (index.astype(jnp.float32) + 0.5) * width(e, done) - 0.5 * GRID


def wave(position):
    y = -position
    t = y * y
    first = y * (3.14159265 + t * (-5.16771278 + t * (2.55016404 + t * (-0.599264529 + t * (0.0821458866 - t * 0.00737043)))))
    double = first * first
    return 1.0, first, 2.0 * double - 1.0, first * (4.0 * double - 3.0)


def speed(modes, px, py):
    wx, wy = wave(px), wave(py)
    total = None
    for j in range(MODES):
        row = modes[j, 0] + modes[j, 1] * wy[1]
        for k in range(2, MODES):
            row = row + modes[j, k] * wy[k]
        row = row * wx[j] if j else row
        total = row if total is None else total + row
    return total + 0.3


def coords():
    sx, sy = lax.axis_index("sx"), lax.axis_index("sy")
    return sx // 8, sx // 2 % 4, sy // 2 * 2 + sx % 2, sy % 2


def device(x, y, z, c):
    return ((x * 4 + y) * 2 + z % 2, z // 2 * 2 + c)


def slot_of(z):
    return z % 2 * 4 + z // 2


def kernel(w_ref, modes, out_ref, given, packed, first, both, work, swapped, ready, last, table, final, local_sem,
           a_send, a_recv, c_send, c_recv, x_send, x_recv, o_send, o_recv):
    x, y, z, c = coords()
    lane = lax.broadcasted_iota(jnp.int32, TILE, 1)
    sub = lax.broadcasted_iota(jnp.int32, TILE, 0)
    low = lane < 64
    half_turn = functools.partial(pltpu.roll, shift=64, axis=1)

    load = pltpu.make_async_copy(w_ref, given, local_sem.at[0])
    load.start()
    barrier = pltpu.get_barrier_semaphore()

    @pl.loop(1, 32)
    def _(d):
        to = device(x, (y + d // 8) % 4, (z + d) % 8, c)
        pl.semaphore_signal(barrier, inc=1, device_id=to, device_id_type=MESH)

    for d in range(1, 4):
        pl.semaphore_signal(barrier, inc=1, device_id=device((x + d) % 4, y, z, c), device_id_type=MESH)
    pl.semaphore_signal(barrier, inc=1, device_id=device(x, y, z, 1 - c), device_id_type=MESH)

    load.wait()

    @pl.loop(0, 32)
    def _(k):
        for jt in range(4):
            re, im = given[0, k, jt], given[1, k, jt]
            packed[0, k, jt * 8 : jt * 8 + 8] = jnp.where(low, re, half_turn(im))
            packed[1, k, jt * 8 : jt * 8 + 8] = jnp.where(low, half_turn(re), im)

    pl.semaphore_wait(barrier, 35)

    me = y * 8 + slot_of(z)

    def first_copy(q, d):
        ty, tz = (y + d // 8) % 4, (z + d) % 8
        return pltpu.make_async_remote_copy(
            src_ref=packed.at[q, :, ty * 8 + tz],
            dst_ref=first.at[q, :, me],
            send_sem=a_send.at[q, d],
            recv_sem=a_recv.at[q, me],
            device_id=device(x, ty, tz, c),
            device_id_type=MESH,
        )

    for q in range(2):

        @pl.loop(1, 32)
        def _(d):
            first_copy(q, d).start()

        pltpu.make_async_copy(packed.at[q, :, y * 8 + z], first.at[q, :, me], a_recv.at[q, me]).start()

    def first_wait(q):
        @pl.loop(0, 32)
        def _(s):
            pltpu.make_async_copy(first.at[q, :, s], first.at[q, :, s], a_recv.at[q, s]).wait()

    def position(phase, tile):
        zh = sub & 3
        if phase == 0:
            return x * 8 + (lane >> 6) * 4 + tile * 2 + (sub >> 2), zh * 2 + c
        return tile * 16 + (sub >> 2) * 8 + (lane >> 6) * 4 + x, zh * 2 + c

    high = ((lane >> 4) & 3, lane & 15)
    chunk = y * 8 + z
    starts = [(chunk // 4, chunk % 4 * 2 + q) for q in range(2)]

    def spot(phase, tile, q, done):
        at = position(phase, tile)
        return [place(starts[q][e], at[e], done[e]) for e in range(2)]

    def make_table(n):
        e, dx, dy = LEVELS[n]
        done = (dx, dy)
        after = (dx + 1, dy) if e == 0 else (dx, dy + 1)
        phase = 0 if n < 6 else 1
        exact = n == 0
        h = [0.5 * width(i, done[i]) for i in range(2)]
        wide = n in (0, 1, 6)
        factor, inner, outer, base = {}, {}, {}, {}
        for tile in range(2):
            at = position(phase, tile)
            for q in range(2):
                new = spot(phase, tile, q, after)
                sp_new = speed(modes, *new)
                base[q, tile] = (new, sp_new)
                if n == 0:
                    factor[q, tile] = sp_new
                    outer[q, tile] = new[0] * h[0]
                    inner[q, tile] = new[1] * h[1]
                else:
                    old = spot(phase, tile, q, done)
                    factor[q, tile] = sp_new - speed(modes, *old)
                    outer[q, tile] = (new[e] - old[e]) * h[e]
        other = 1 - e
        for child in range(2):
            freq = {}
            for tile in range(2 if wide else 1):
                at = list(position(phase, tile))
                parent = [middle(i, high[i], at[i], after[i]) for i in range(2)]
                at[e] = ((at[e] >> (done[e] + 1)) * 2 + child) << done[e]
                mid = [middle(i, high[i], at[i], done[i]) for i in range(2)]
                square = 1.0 + mid[0] * mid[0] + mid[1] * mid[1]
                root = jnp.sqrt(square)
                root_parent = jnp.sqrt(1.0 + parent[0] * parent[0] + parent[1] * parent[1])
                v = (child - 0.5) * 2.0 * h[e]
                step = v * (v + 2.0 * parent[e]) / (root + root_parent)
                freq[tile] = (mid, square, root, v, step)
            constant = {}
            for tile in range(2):
                mid, square, root, v, step = freq[tile if wide else 0]
                for q in range(2):
                    new, sp_new = base[q, tile]
                    constant[q, tile] = frac(new[e] * v) + frac(sp_new * step)

            @pl.loop(0, CHEB[e])
            def _(ko):
                zo = node(e, ko)
                uo = zo * h[e]
                shift = {key: constant[key] + outer[key] * zo for key in constant}
                first_part = {t: uo * (uo + 2.0 * freq[t][0][e]) for t in freq}
                for ki in range(CHEB[other]):
                    ui = float(NODES[other][ki]) * h[other]
                    delta = {}
                    for t in freq:
                        mid, square, root = freq[t][:3]
                        total = first_part[t] + ui * (ui + 2.0 * mid[other])
                        near = square + total
                        if exact:
                            delta[t] = total / (jnp.sqrt(near) + root)
                        else:
                            delta[t] = total * pl.reciprocal(near * lax.rsqrt(near) + root, approx=True)
                    for tile in range(2):
                        for q in range(2):
                            angle = delta[tile if wide else 0] * factor[q, tile] + shift[q, tile]
                            if n == 0:
                                angle = angle + inner[q, tile] * float(NODES[other][ki])
                            cos, sin = turn(angle)
                            k = (ko, ki) if e == 0 else (ki, ko)
                            table[n, q, tile, child, k[0], k[1], 0] = cos
                            table[n, q, tile, child, k[0], k[1], 1] = sin

    def make_final():
        done = (5, 3)
        h = [0.5 * width(i, done[i]) for i in range(2)]
        at = position(1, 0)
        mid = [middle(i, high[i], at[i], done[i]) for i in range(2)]
        square = 1.0 + mid[0] * mid[0] + mid[1] * mid[1]
        root = jnp.sqrt(square)
        here = {}
        for tile in range(2):
            for q in range(2):
                px, py = spot(1, tile, q, done)
                here[q, tile] = (px * h[0], py * h[1], speed(modes, px, py))

        @pl.loop(0, CHEB[0])
        def _(ko):
            zo = node(0, ko)
            uo = zo * h[0]
            shift = {key: frac(here[key][0] * zo) for key in here}
            first_part = uo * (uo + 2.0 * mid[0])
            for ki in range(CHEB[1]):
                zi = float(NODES[1][ki])
                ui = zi * h[1]
                total = first_part + ui * (ui + 2.0 * mid[1])
                delta = total / (jnp.sqrt(square + total) + root)
                for tile in range(2):
                    for q in range(2):
                        angle = shift[q, tile] + frac(here[q, tile][1] * zi) + frac(here[q, tile][2] * delta)
                        cos, sin = turn(angle)
                        final[q, tile, ko, ki, 0] = cos
                        final[q, tile, ko, ki, 1] = sin

    def children(how, own):
        if how == "tile":
            return [(own[0], own[1])] * 2
        axis, bit, size = how
        bit_set = ((sub if axis == 0 else lane) & bit) != 0
        result = []
        for value in own:
            up = pltpu.roll(value, bit, axis)
            down = up if 2 * bit == size else pltpu.roll(value, size - bit, axis)
            result.append((jnp.where(bit_set, up, value), jnp.where(bit_set, value, down)))
        return result

    def level(n, q, how, read, write):
        e = LEVELS[n][0]
        size = CHEB[e]

        @pl.loop(0, CHEB[1 - e])
        def _(ko):
            at = [(k, ko) if e == 0 else (ko, k) for k in range(size)]
            sums = {}
            values = [read(*k) for k in at]
            for tile in range(2):
                parts = [[[], []], [[], []]]
                for i, k in enumerate(at):
                    if how is None:
                        pair_re, pair_im = values[i][tile]
                    else:
                        pair_re = children(how, values[i][0])[tile] if how == "tile" else children(how, [values[i][0][tile]])[0]
                        pair_im = children(how, values[i][1])[tile] if how == "tile" else children(how, [values[i][1][tile]])[0]
                    for child in range(2):
                        cos = table[n, q, tile, child, k[0], k[1], 0]
                        sin = table[n, q, tile, child, k[0], k[1], 1]
                        re, im = pair_re[child], pair_im[child]
                        parts[child][0].append(cos * re - sin * im)
                        parts[child][1].append(sin * re + cos * im)
                sums[tile] = [merge(size, parts[0][r], parts[1][r]) for r in range(2)]
            for tile in range(2):
                for i, k in enumerate(at):
                    write(k[0], k[1], tile, sums[tile][0][i], sums[tile][1][i])

    def read_first(q):
        def read(k0, k1):
            blocks = [first[q, k0 * 8 + k1, t * 8 : t * 8 + 8] for t in range(4)]
            turned = [half_turn(b) for b in blocks]
            re = [jnp.where(low, blocks[t], turned[2 + t]) for t in range(2)]
            im = [jnp.where(low, turned[t], blocks[2 + t]) for t in range(2)]
            return re, im

        return read

    def reader(ref, q):
        return lambda k0, k1: [[ref[q, r, k0, k1, t] for t in range(2)] for r in range(2)]

    def writer(ref, q):
        def write(k0, k1, tile, re, im):
            ref[q, 0, k0, k1, tile] = re
            ref[q, 1, k0, k1, tile] = im

        return write

    def write_both(q):
        def write(k0, k1, tile, re, im):
            both[q, c, 0, k0, k1, tile] = re
            both[q, c, 1, k0, k1, tile] = im

        return write

    def read_both(q):
        def read(k0, k1):
            return [[[both[q, child, r, k0, k1, t] for child in range(2)] for r in range(2)] for t in range(2)]

        return read

    def write_ready(q):
        def write(k0, k1, tile, re, im):
            cos, sin = final[q, tile, k0, k1, 0], final[q, tile, k0, k1, 1]
            re, im = cos * re + sin * im, cos * im - sin * re
            ready[q, 0, k0 * 8 + k1, tile * 8 : tile * 8 + 8] = jnp.where(low, re, half_turn(im))
            ready[q, 1, k0 * 8 + k1, tile * 8 : tile * 8 + 8] = jnp.where(low, half_turn(re), im)

        return write

    def core_copy(q):
        return pltpu.make_async_remote_copy(
            src_ref=both.at[q, c],
            dst_ref=both.at[q, c],
            send_sem=c_send.at[q],
            recv_sem=c_recv.at[q],
            device_id=device(x, y, z, 1 - c),
            device_id_type=MESH,
        )

    def group(q, g):
        return work.at[q, :, :, :, g // 2, pl.ds(g % 2 * 4, 4)]

    def arrived(q, g):
        return swapped.at[q, :, :, :, g // 2, pl.ds(g % 2 * 4, 4)]

    def x_copy(q, d):
        t = (x + d) % 4
        return pltpu.make_async_remote_copy(
            src_ref=group(q, t),
            dst_ref=arrived(q, x),
            send_sem=x_send.at[q, d],
            recv_sem=x_recv.at[q, x],
            device_id=device(t, y, z, c),
            device_id_type=MESH,
        )

    def x_start(q):
        for d in (2, 1, 3):
            x_copy(q, d).start()
        pltpu.make_async_copy(group(q, x), arrived(q, x), x_recv.at[q, x]).start()

    def x_wait(q):
        @pl.loop(0, 4)
        def _(g):
            pltpu.make_async_copy(arrived(q, g), arrived(q, g), x_recv.at[q, g]).wait()

    target_x = x

    def last_copy(q, d):
        tx, ty1, tz1 = (target_x + d // 8) % 4, (y // 2 + d // 4) % 2, (z // 2 + d) % 4
        to = device(tx, ty1 * 2 + x // 2, tz1 * 2 + x % 2, c)
        return ready.at[q, ty1, :, tx * 4 + tz1], to

    own_y1, own_z1 = y // 2, z // 2

    def start_last(q):
        mine = jnp.logical_and(y % 2 == x // 2, z % 2 == x % 2)

        @pl.loop(0, 32)
        def _(d):
            src, to = last_copy(q, d)
            dst = last.at[q, :, chunk]

            @pl.when(jnp.logical_not(jnp.logical_and(mine, d == 0)))
            def _():
                pltpu.make_async_remote_copy(
                    src_ref=src, dst_ref=dst, send_sem=o_send.at[q, d], recv_sem=o_recv.at[q, chunk],
                    device_id=to, device_id_type=MESH,
                ).start()

            @pl.when(jnp.logical_and(mine, d == 0))
            def _():
                pltpu.make_async_copy(src, dst, o_recv.at[q, chunk]).start()

    def wait_last_sends(q):
        mine = jnp.logical_and(y % 2 == x // 2, z % 2 == x % 2)

        @pl.loop(0, 32)
        def _(d):
            @pl.when(jnp.logical_not(jnp.logical_and(mine, d == 0)))
            def _():
                pltpu.make_async_copy(last.at[q, :, 0], last.at[q, :, 0], o_send.at[q, d]).wait()

    def wait_last(q):
        @pl.loop(0, 32)
        def _(s):
            pltpu.make_async_copy(last.at[q, :, s], last.at[q, :, s], o_recv.at[q, s]).wait()

    z0, z1, z2, y1 = (0, 4, 8), (0, 1, 8), (0, 2, 8), (1, 64, 128)

    def start_mid(q):
        first_wait(q)
        level(0, q, z0, read_first(q), write_both(q))
        core_copy(q).start()

    def mid(q):
        core_copy(q).wait()
        level(1, q, None, read_both(q), writer(work, q))
        level(2, q, "tile", reader(work, q), writer(work, q))
        level(3, q, z1, reader(work, q), writer(work, q))
        level(4, q, y1, reader(work, q), writer(work, q))
        level(5, q, z2, reader(work, q), writer(work, q))
        x_start(q)

    def end_mid(q):
        x_wait(q)
        level(6, q, z0, reader(swapped, q), writer(swapped, q))
        level(7, q, "tile", reader(swapped, q), write_ready(q))
        start_last(q)

    for n in range(6):
        make_table(n)
    start_mid(0)
    make_table(6)
    mid(0)
    make_table(7)
    make_final()
    end_mid(0)
    start_mid(1)
    mid(1)
    end_mid(1)

    for q in range(2):
        wait_last(q)

    @pl.loop(0, 32)
    def _(k):
        for jt in range(4):
            zero, one = last[0, k, jt * 8 : jt * 8 + 8], last[1, k, jt * 8 : jt * 8 + 8]
            out_ref[0, k, jt] = jnp.where(low, zero, half_turn(one))
            out_ref[1, k, jt] = jnp.where(low, half_turn(zero), one)

    for q in range(2):

        @pl.loop(1, 32)
        def _(d):
            first_copy(q, d).wait_send()

        for d in range(1, 4):
            x_copy(q, d).wait_send()
        wait_last_sends(q)


def body(weights_in, speed_modes):
    half = (2, 2, 4, 8, 2, *TILE)
    f32 = jnp.float32
    out = pl.pallas_call(
        kernel,
        out_shape=jax.ShapeDtypeStruct((2, 32, 4, *TILE), f32),
        in_specs=[pl.BlockSpec(memory_space=pltpu.HBM), pl.BlockSpec(memory_space=pltpu.SMEM)],
        out_specs=pl.BlockSpec(memory_space=pltpu.VMEM),
        scratch_shapes=[
            pltpu.VMEM((2, 32, 4, *TILE), f32),
            pltpu.VMEM((2, 32, 32, 128), f32),
            pltpu.VMEM((2, 32, 32, 128), f32),
            pltpu.VMEM((2, *half), f32),
            pltpu.VMEM(half, f32),
            pltpu.VMEM(half, f32),
            pltpu.VMEM((2, 2, 32, 16, 128), f32),
            pltpu.VMEM((2, 32, 32, 128), f32),
            pltpu.VMEM((8, 2, 2, 2, 4, 8, 2, *TILE), f32),
            pltpu.VMEM((2, 2, 4, 8, 2, *TILE), f32),
            pltpu.SemaphoreType.DMA((1,)),
            pltpu.SemaphoreType.DMA((2, 32)),
            pltpu.SemaphoreType.DMA((2, 32)),
            pltpu.SemaphoreType.DMA((2,)),
            pltpu.SemaphoreType.DMA((2,)),
            pltpu.SemaphoreType.DMA((2, 4)),
            pltpu.SemaphoreType.DMA((2, 4)),
            pltpu.SemaphoreType.DMA((2, 32)),
            pltpu.SemaphoreType.DMA((2, 32)),
        ],
        compiler_params=pltpu.CompilerParams(collective_id=0, has_side_effects=True, vmem_limit_bytes=48 << 20),
    )(weights_in.reshape(2, 32, 4, *TILE), speed_modes)
    return out.reshape(weights_in.shape)


def solution(mesh):
    placed = P(None, None, "sx", "sy", None)
    return jax.shard_map(body, mesh=mesh, in_specs=(placed, P()), out_specs=placed, check_vma=False)
```

```python
import functools

import jax
import jax.numpy as jnp
import numpy as np
from jax import lax
from jax.experimental import pallas as pl
from jax.experimental.pallas import tpu as pltpu
from jax.sharding import PartitionSpec as P

MESH = pl.DeviceIdType.MESH
GRID = 8192
CHEB = (4, 8)
SPAT = 8
FREQ = (4, 16)
COUNT = (32, 8)
MODES = 4
TILE = (8, 128)
LEVELS = ((0, 0, 0), (1, 1, 0), (0, 1, 1), (1, 2, 1), (0, 2, 2), (1, 3, 2), (0, 3, 3), (0, 4, 3))
SIN_POLY = (4.44288292, -7.30824569, 3.60635422, -0.84611165, 0.10982452)
COS_POLY = (1.4142135, -6.97885095, 5.73946038, -1.88355791, 0.31068803)


def cheb_nodes(q):
    return np.cos((2.0 * np.arange(q) + 1.0) * np.pi / (2.0 * q))


NODES = tuple(np.asarray(cheb_nodes(q), np.float32).astype(np.float64) for q in CHEB)


def child_table(q):
    z = cheb_nodes(q)
    points = -0.5 + 0.5 * z
    table = np.ones((q, q))
    for k in range(q):
        for j in range(q):
            if j != k:
                table[k, :] *= (points - z[j]) / (z[k] - z[j])
    return table


def halves(q):
    table = child_table(q)
    even = 0.5 * (table + table[::-1])[: q // 2]
    odd = 0.5 * (table - table[::-1])[: q // 2]
    return even, odd


HALVES = tuple(halves(q) for q in CHEB)


def merge(q, a, b):
    even, odd = HALVES[0 if q == 4 else 1]
    plus = [a[k] + b[q - 1 - k] for k in range(q)]
    minus = [a[k] - b[q - 1 - k] for k in range(q)]
    out = [None] * q
    for k in range(q // 2):
        e = plus[0] * float(even[k, 0])
        o = minus[0] * float(odd[k, 0])
        for j in range(1, q):
            e = e + plus[j] * float(even[k, j])
            o = o + minus[j] * float(odd[k, j])
        out[k] = e + o
        out[q - 1 - k] = e - o
    return out


def frac(v):
    return v - jnp.round(v)


def poly(coefficients, t):
    result = t * coefficients[-1] + coefficients[-2]
    for value in coefficients[-3::-1]:
        result = result * t + value
    return result


def turn(angle):
    r = frac(angle)
    t = r * r
    s = poly(SIN_POLY, t) * r
    c = poly(COS_POLY, t)
    return 1.0 - s * s, s * c


def node(e, k):
    value = jnp.float32(NODES[e][0])
    for i in range(1, CHEB[e]):
        value = jnp.where(k == i, jnp.float32(NODES[e][i]), value)
    return value


def rev(v, bits):
    result = jnp.int32(0)
    for t in range(bits):
        result = result + ((v >> t) & 1) * (1 << (bits - 1 - t))
    return result


def place(start, coord, done):
    index = start * (1 << done) + rev(coord, done)
    return (index.astype(jnp.float32) + 0.5) * (1.0 / (SPAT << done)) - 0.5


def width(e, done):
    return float(GRID // (FREQ[e] * COUNT[e]) * (1 << done))


def middle(e, high, coord, done):
    index = high * (COUNT[e] >> done) + (coord >> done)
    return (index.astype(jnp.float32) + 0.5) * width(e, done) - 0.5 * GRID


def wave(position):
    y = -position
    t = y * y
    first = y * (3.14159265 + t * (-5.16771278 + t * (2.55016404 + t * (-0.599264529 + t * (0.0821458866 - t * 0.00737043)))))
    double = first * first
    return 1.0, first, 2.0 * double - 1.0, first * (4.0 * double - 3.0)


def speed(modes, px, py):
    wx, wy = wave(px), wave(py)
    total = None
    for j in range(MODES):
        row = modes[j, 0] + modes[j, 1] * wy[1]
        for k in range(2, MODES):
            row = row + modes[j, k] * wy[k]
        row = row * wx[j] if j else row
        total = row if total is None else total + row
    return total + 0.3


def coords():
    sx, sy = lax.axis_index("sx"), lax.axis_index("sy")
    return sx >> 3, (sx >> 1) & 3, (sy >> 1) * 2 + (sx & 1), sy & 1


def device(x, y, z, c):
    return ((x * 4 + y) * 2 + (z & 1), (z >> 1) * 2 + c)


def slot_of(z):
    return (z & 1) * 4 + (z >> 1)


def kernel(w_ref, modes, out_ref, packed, first, both, work, swapped, ready, last, table, final,
           a_send, a_recv, c_send, c_recv, x_send, x_recv, o_send, o_recv):
    x, y, z, c = coords()
    lane = lax.broadcasted_iota(jnp.int32, TILE, 1)
    sub = lax.broadcasted_iota(jnp.int32, TILE, 0)
    low = lane < 64
    half_turn = functools.partial(pltpu.roll, shift=64, axis=1)

    barrier = pltpu.get_barrier_semaphore()

    for d in range(1, 32):
        to = device(x, (y + (d >> 3)) & 3, (z + d) & 7, c)
        pl.semaphore_signal(barrier, inc=1, device_id=to, device_id_type=MESH)

    for d in range(1, 4):
        pl.semaphore_signal(barrier, inc=1, device_id=device((x + d) & 3, y, z, c), device_id_type=MESH)
    pl.semaphore_signal(barrier, inc=1, device_id=device(x, y, z, 1 - c), device_id_type=MESH)

    @pl.loop(0, 32)
    def _(k):
        for jt in range(4):
            re, im = w_ref[0, k, jt], w_ref[1, k, jt]
            packed[0, k, jt * 8 : jt * 8 + 8] = jnp.where(low, re, half_turn(im))
            packed[1, k, jt * 8 : jt * 8 + 8] = jnp.where(low, half_turn(re), im)

    pl.semaphore_wait(barrier, 35)

    me = y * 8 + slot_of(z)

    def first_copy(q, d):
        ty, tz = (y + (d >> 3)) & 3, (z + d) & 7
        return pltpu.make_async_remote_copy(
            src_ref=packed.at[q, :, ty * 8 + tz],
            dst_ref=first.at[q, :, me],
            send_sem=a_send.at[q, d],
            recv_sem=a_recv.at[q, me],
            device_id=device(x, ty, tz, c),
            device_id_type=MESH,
        )

    def first_start(q, begin, count):
        for d in range(count):
            first_copy(q, begin + d).start()

    def first_own(q):
        pltpu.make_async_copy(packed.at[q, :, y * 8 + z], first.at[q, :, me], a_recv.at[q, me]).start()

    def first_sent(q):
        @pl.loop(1, 32)
        def _(d):
            first_copy(q, d).wait_send()

    first_start(0, 1, 31)
    first_start(1, 1, 31)
    first_own(0)
    first_own(1)

    def first_wait(q):
        @pl.loop(0, 32)
        def _(s):
            pltpu.make_async_copy(first.at[q, :, s], first.at[q, :, s], a_recv.at[q, s]).wait()

    def group_of(to):
        return (((to >> 1) + y) & 1) * 2 + ((to + z) & 1)

    mine = group_of(x)

    def position(phase, tile):
        zh = sub & 3
        if phase == 0:
            return x * 8 + (lane >> 6) * 4 + tile * 2 + (sub >> 2), zh * 2 + c
        return tile * 16 + (sub >> 2) * 8 + (lane >> 6) * 4 + mine, zh * 2 + c

    high = ((lane >> 4) & 3, lane & 15)
    chunk = y * 8 + z
    starts = [(chunk // 4, chunk % 4 * 2 + q) for q in range(2)]

    def spot(phase, tile, q, done):
        at = position(phase, tile)
        return [place(starts[q][e], at[e], done[e]) for e in range(2)]

    def make_table(n):
        e, dx, dy = LEVELS[n]
        done = (dx, dy)
        after = (dx + 1, dy) if e == 0 else (dx, dy + 1)
        phase = 0 if n < 6 else 1
        exact = n == 0
        h = [0.5 * width(i, done[i]) for i in range(2)]
        wide = n in (0, 1, 6)
        factor, inner, outer, base = {}, {}, {}, {}
        for tile in range(2):
            at = position(phase, tile)
            for q in range(2):
                new = spot(phase, tile, q, after)
                sp_new = speed(modes, *new)
                base[q, tile] = (new, sp_new)
                if n == 0:
                    factor[q, tile] = sp_new
                    outer[q, tile] = new[0] * h[0]
                    inner[q, tile] = new[1] * h[1]
                else:
                    old = spot(phase, tile, q, done)
                    factor[q, tile] = sp_new - speed(modes, *old)
                    outer[q, tile] = (new[e] - old[e]) * h[e]
        other = 1 - e
        for child in range(2):
            freq = {}
            for tile in range(2 if wide else 1):
                at = list(position(phase, tile))
                parent = [middle(i, high[i], at[i], after[i]) for i in range(2)]
                at[e] = ((at[e] >> (done[e] + 1)) * 2 + child) << done[e]
                mid = [middle(i, high[i], at[i], done[i]) for i in range(2)]
                square = 1.0 + mid[0] * mid[0] + mid[1] * mid[1]
                root = jnp.sqrt(square)
                root_parent = jnp.sqrt(1.0 + parent[0] * parent[0] + parent[1] * parent[1])
                v = (child - 0.5) * 2.0 * h[e]
                step = v * (v + 2.0 * parent[e]) / (root + root_parent)
                freq[tile] = (mid, square, root, v, step)
            constant = {}
            for tile in range(2):
                mid, square, root, v, step = freq[tile if wide else 0]
                for q in range(2):
                    new, sp_new = base[q, tile]
                    constant[q, tile] = frac(new[e] * v) + frac(sp_new * step)

            @pl.loop(0, CHEB[e])
            def _(ko):
                zo = node(e, ko)
                uo = zo * h[e]
                shift = {key: constant[key] + outer[key] * zo for key in constant}
                first_part = {t: uo * (uo + 2.0 * freq[t][0][e]) for t in freq}
                for ki in range(CHEB[other]):
                    ui = float(NODES[other][ki]) * h[other]
                    delta = {}
                    for t in freq:
                        mid, square, root = freq[t][:3]
                        total = first_part[t] + ui * (ui + 2.0 * mid[other])
                        near = square + total
                        if exact:
                            delta[t] = total / (jnp.sqrt(near) + root)
                        else:
                            delta[t] = total * pl.reciprocal(near * lax.rsqrt(near) + root, approx=True)
                    for tile in range(2):
                        for q in range(2):
                            angle = delta[tile if wide else 0] * factor[q, tile] + shift[q, tile]
                            if n == 0:
                                angle = angle + inner[q, tile] * float(NODES[other][ki])
                            cos, sin = turn(angle)
                            k = (ko, ki) if e == 0 else (ki, ko)
                            table[n, q, tile, child, k[0], k[1], 0] = cos
                            table[n, q, tile, child, k[0], k[1], 1] = sin

    def make_final():
        done = (5, 3)
        h = [0.5 * width(i, done[i]) for i in range(2)]
        at = position(1, 0)
        mid = [middle(i, high[i], at[i], done[i]) for i in range(2)]
        square = 1.0 + mid[0] * mid[0] + mid[1] * mid[1]
        root = jnp.sqrt(square)
        here = {}
        for tile in range(2):
            for q in range(2):
                px, py = spot(1, tile, q, done)
                here[q, tile] = (px * h[0], py * h[1], speed(modes, px, py))

        @pl.loop(0, CHEB[0])
        def _(ko):
            zo = node(0, ko)
            uo = zo * h[0]
            shift = {key: frac(here[key][0] * zo) for key in here}
            first_part = uo * (uo + 2.0 * mid[0])
            for ki in range(CHEB[1]):
                zi = float(NODES[1][ki])
                ui = zi * h[1]
                total = first_part + ui * (ui + 2.0 * mid[1])
                delta = total / (jnp.sqrt(square + total) + root)
                for tile in range(2):
                    for q in range(2):
                        angle = shift[q, tile] + frac(here[q, tile][1] * zi) + frac(here[q, tile][2] * delta)
                        cos, sin = turn(angle)
                        final[q, tile, ko, ki, 0] = cos
                        final[q, tile, ko, ki, 1] = sin

    def children(how, own):
        if how == "tile":
            return [(own[0], own[1])] * 2
        axis, bit, size = how
        bit_set = ((sub if axis == 0 else lane) & bit) != 0
        result = []
        for value in own:
            up = pltpu.roll(value, bit, axis)
            down = up if 2 * bit == size else pltpu.roll(value, size - bit, axis)
            result.append((jnp.where(bit_set, up, value), jnp.where(bit_set, value, down)))
        return result

    def level(n, q, how, read, write, then=None):
        e = LEVELS[n][0]
        size = CHEB[e]

        @pl.loop(0, CHEB[1 - e])
        def _(ko):
            at = [(k, ko) if e == 0 else (ko, k) for k in range(size)]
            sums = {}
            values = [read(*k) for k in at]
            for tile in range(2):
                parts = [[[], []], [[], []]]
                for i, k in enumerate(at):
                    if how is None:
                        pair_re, pair_im = values[i][tile]
                    else:
                        pair_re = children(how, values[i][0])[tile] if how == "tile" else children(how, [values[i][0][tile]])[0]
                        pair_im = children(how, values[i][1])[tile] if how == "tile" else children(how, [values[i][1][tile]])[0]
                    for child in range(2):
                        cos = table[n, q, tile, child, k[0], k[1], 0]
                        sin = table[n, q, tile, child, k[0], k[1], 1]
                        re, im = pair_re[child], pair_im[child]
                        parts[child][0].append(cos * re - sin * im)
                        parts[child][1].append(sin * re + cos * im)
                sums[tile] = [merge(size, parts[0][r], parts[1][r]) for r in range(2)]
            for tile in range(2):
                for i, k in enumerate(at):
                    write(k[0], k[1], tile, sums[tile][0][i], sums[tile][1][i])
            if then is not None:
                then(ko)

    def read_first(q):
        def read(k0, k1):
            blocks = [first[q, k0 * 8 + k1, t * 8 : t * 8 + 8] for t in range(4)]
            turned = [half_turn(b) for b in blocks]
            re = [jnp.where(low, blocks[t], turned[2 + t]) for t in range(2)]
            im = [jnp.where(low, turned[t], blocks[2 + t]) for t in range(2)]
            return re, im

        return read

    def reader(ref, q):
        return lambda k0, k1: [[ref[q, r, k0, k1, t] for t in range(2)] for r in range(2)]

    def writer(ref, q):
        def write(k0, k1, tile, re, im):
            ref[q, 0, k0, k1, tile] = re
            ref[q, 1, k0, k1, tile] = im

        return write

    def write_both(q):
        def write(k0, k1, tile, re, im):
            both[q, c, 0, k0, k1, tile] = re
            both[q, c, 1, k0, k1, tile] = im

        return write

    def read_both(q):
        def read(k0, k1):
            return [[[both[q, child, r, k0, k1, t] for child in range(2)] for r in range(2)] for t in range(2)]

        return read

    def write_ready(q):
        def write(k0, k1, tile, re, im):
            cos, sin = final[q, tile, k0, k1, 0], final[q, tile, k0, k1, 1]
            re, im = cos * re + sin * im, cos * im - sin * re
            ready[q, 0, k0 * 8 + k1, tile * 8 : tile * 8 + 8] = jnp.where(low, re, half_turn(im))
            ready[q, 1, k0 * 8 + k1, tile * 8 : tile * 8 + 8] = jnp.where(low, half_turn(re), im)

        return write

    def core_copy(q):
        return pltpu.make_async_remote_copy(
            src_ref=both.at[q, c],
            dst_ref=both.at[q, c],
            send_sem=c_send.at[q],
            recv_sem=c_recv.at[q],
            device_id=device(x, y, z, 1 - c),
            device_id_type=MESH,
        )

    def group(q, g, k0):
        return work.at[q, :, k0, :, g >> 1, pl.ds((g & 1) * 4, 4)]

    def arrived(q, g, k0):
        return swapped.at[q, :, k0, :, g >> 1, pl.ds((g & 1) * 4, 4)]

    def x_copy(q, d, k0):
        t = (x + d) & 3
        return pltpu.make_async_remote_copy(
            src_ref=group(q, group_of(t), k0),
            dst_ref=arrived(q, x, k0),
            send_sem=x_send.at[q, d, k0],
            recv_sem=x_recv.at[q, x, k0],
            device_id=device(t, y, z, c),
            device_id_type=MESH,
        )

    def x_wait(q):
        @pl.loop(0, 16)
        def _(i):
            part = arrived(q, i >> 2, i & 3)
            pltpu.make_async_copy(part, part, x_recv.at[q, i >> 2, i & 3]).wait()

    def last_copy(q, d):
        tx, ty1, tz1 = (x + (d >> 3)) & 3, ((y >> 1) + (d >> 2)) & 1, ((z >> 1) + d) & 3
        to = device(tx, ty1 * 2 + (mine >> 1), tz1 * 2 + (mine & 1), c)
        return ready.at[q, ty1, :, tx * 4 + tz1], to

    def last_remote(q, d):
        src, to = last_copy(q, d)
        return pltpu.make_async_remote_copy(
            src_ref=src,
            dst_ref=last.at[q, :, chunk],
            send_sem=o_send.at[q, d],
            recv_sem=o_recv.at[q, chunk],
            device_id=to,
            device_id_type=MESH,
        )

    def start_last(q, begin, count):
        for d in range(count):
            last_remote(q, begin + d).start()

    def start_last_own(q):
        @pl.when(x != 0)
        def _():
            last_remote(q, 0).start()

        @pl.when(x == 0)
        def _():
            pltpu.make_async_copy(last_copy(q, 0)[0], last.at[q, :, chunk], o_recv.at[q, chunk]).start()

    def wait_last_sends(q):
        @pl.loop(1, 32)
        def _(d):
            last_remote(q, d).wait_send()

        @pl.when(x != 0)
        def _():
            last_remote(q, 0).wait_send()

    def wait_last(q):
        @pl.loop(0, 32)
        def _(s):
            pltpu.make_async_copy(last.at[q, :, s], last.at[q, :, s], o_recv.at[q, s]).wait()

    z0, z1, z2, y1 = (0, 4, 8), (0, 1, 8), (0, 2, 8), (1, 64, 128)

    def open_half(q):
        first_wait(q)
        level(0, q, z0, read_first(q), write_both(q))
        core_copy(q).start()

    def middle_half(q):
        core_copy(q).wait()
        level(1, q, None, read_both(q), writer(work, q))
        level(2, q, "tile", reader(work, q), writer(work, q))
        level(3, q, z1, reader(work, q), writer(work, q))
        level(4, q, y1, reader(work, q), writer(work, q))

    def swap_half(q, more, done, each):
        def send(k0):
            for n, d in enumerate((2, 1, 3)):
                x_copy(q, d, k0).start()
                begin, end = n * each // 3, (n + 1) * each // 3
                more(done + k0 * each + begin, end - begin)
            pltpu.make_async_copy(group(q, mine, k0), arrived(q, x, k0), x_recv.at[q, x, k0]).start()

        level(5, q, z2, reader(work, q), writer(work, q), send)

    def second_half(q):
        x_wait(q)
        level(6, q, z0, reader(swapped, q), writer(swapped, q))
        level(7, q, "tile", reader(swapped, q), write_ready(q))

    for n in range(8):
        make_table(n)
    make_final()
    open_half(0)
    middle_half(0)
    swap_half(0, (lambda b, n: None), 0, 0)
    open_half(1)
    middle_half(1)
    swap_half(1, (lambda b, n: None), 0, 0)
    second_half(0)
    start_last(0, 1, 31)
    start_last_own(0)
    second_half(1)
    start_last(1, 1, 31)
    start_last_own(1)
    for q in range(2):
        wait_last(q)

    @pl.loop(0, 32)
    def _(k):
        for jt in range(4):
            zero, one = last[0, k, jt * 8 : jt * 8 + 8], last[1, k, jt * 8 : jt * 8 + 8]
            out_ref[0, k, jt] = jnp.where(low, zero, half_turn(one))
            out_ref[1, k, jt] = jnp.where(low, half_turn(zero), one)

    for q in range(2):
        first_sent(q)
        for d in range(1, 4):
            for k0 in range(4):
                x_copy(q, d, k0).wait_send()
        wait_last_sends(q)


def body(weights_in, speed_modes):
    half = (2, 2, 4, 8, 2, *TILE)
    f32 = jnp.float32
    out = pl.pallas_call(
        kernel,
        out_shape=jax.ShapeDtypeStruct((2, 32, 4, *TILE), f32),
        in_specs=[pl.BlockSpec(memory_space=pltpu.VMEM), pl.BlockSpec(memory_space=pltpu.SMEM)],
        out_specs=pl.BlockSpec(memory_space=pltpu.VMEM),
        scratch_shapes=[
            pltpu.VMEM((2, 32, 32, 128), f32),
            pltpu.VMEM((2, 32, 32, 128), f32),
            pltpu.VMEM((2, *half), f32),
            pltpu.VMEM(half, f32),
            pltpu.VMEM(half, f32),
            pltpu.VMEM((2, 2, 32, 16, 128), f32),
            pltpu.VMEM((2, 32, 32, 128), f32),
            pltpu.VMEM((8, 2, 2, 2, 4, 8, 2, *TILE), f32),
            pltpu.VMEM((2, 2, 4, 8, 2, *TILE), f32),
            pltpu.SemaphoreType.DMA((2, 32)),
            pltpu.SemaphoreType.DMA((2, 32)),
            pltpu.SemaphoreType.DMA((2,)),
            pltpu.SemaphoreType.DMA((2,)),
            pltpu.SemaphoreType.DMA((2, 4, 4)),
            pltpu.SemaphoreType.DMA((2, 4, 4)),
            pltpu.SemaphoreType.DMA((2, 32)),
            pltpu.SemaphoreType.DMA((2, 32)),
        ],
        compiler_params=pltpu.CompilerParams(collective_id=0, has_side_effects=True, vmem_limit_bytes=48 << 20),
    )(weights_in.reshape(2, 32, 4, *TILE), speed_modes)
    return out.reshape(weights_in.shape)


def solution(mesh):
    placed = P(None, None, "sx", "sy", None)
    return jax.shard_map(body, mesh=mesh, in_specs=(placed, P()), out_specs=placed, check_vma=False)
```

```python
import functools

import jax
import jax.numpy as jnp
import numpy as np
from jax import lax
from jax.experimental import pallas as pl
from jax.experimental.pallas import tpu as pltpu
from jax.sharding import PartitionSpec as P

MESH = pl.DeviceIdType.MESH
GRID = 8192
CHEB = (4, 8)
SPAT = 8
FREQ = (4, 16)
COUNT = (32, 8)
MODES = 4
TILE = (8, 128)
LEVELS = ((0, 0, 0), (1, 1, 0), (0, 1, 1), (1, 2, 1), (0, 2, 2), (1, 3, 2), (0, 3, 3), (0, 4, 3))
SIN_POLY = (4.44288292, -7.30824569, 3.60635422, -0.84611165, 0.10982452)
COS_POLY = (1.4142135, -6.97885095, 5.73946038, -1.88355791, 0.31068803)


def cheb_nodes(q):
    return np.cos((2.0 * np.arange(q) + 1.0) * np.pi / (2.0 * q))


NODES = tuple(np.asarray(cheb_nodes(q), np.float32).astype(np.float64) for q in CHEB)


def child_table(q):
    z = cheb_nodes(q)
    points = -0.5 + 0.5 * z
    table = np.ones((q, q))
    for k in range(q):
        for j in range(q):
            if j != k:
                table[k, :] *= (points - z[j]) / (z[k] - z[j])
    return table


def halves(q):
    table = child_table(q)
    even = 0.5 * (table + table[::-1])[: q // 2]
    odd = 0.5 * (table - table[::-1])[: q // 2]
    return even, odd


HALVES = tuple(halves(q) for q in CHEB)


def merge(q, a, b):
    even, odd = HALVES[0 if q == 4 else 1]
    plus = [a[k] + b[q - 1 - k] for k in range(q)]
    minus = [a[k] - b[q - 1 - k] for k in range(q)]
    out = [None] * q
    for k in range(q // 2):
        e = plus[0] * float(even[k, 0])
        o = minus[0] * float(odd[k, 0])
        for j in range(1, q):
            e = e + plus[j] * float(even[k, j])
            o = o + minus[j] * float(odd[k, j])
        out[k] = e + o
        out[q - 1 - k] = e - o
    return out


def frac(v):
    return v - jnp.round(v)


def poly(coefficients, t):
    result = t * coefficients[-1] + coefficients[-2]
    for value in coefficients[-3::-1]:
        result = result * t + value
    return result


def turn(angle):
    r = frac(angle)
    t = r * r
    s = poly(SIN_POLY, t) * r
    c = poly(COS_POLY, t)
    return 1.0 - s * s, s * c


def node(e, k):
    value = jnp.float32(NODES[e][0])
    for i in range(1, CHEB[e]):
        value = jnp.where(k == i, jnp.float32(NODES[e][i]), value)
    return value


def rev(v, bits):
    result = jnp.int32(0)
    for t in range(bits):
        result = result + ((v >> t) & 1) * (1 << (bits - 1 - t))
    return result


def place(start, coord, done):
    index = start * (1 << done) + rev(coord, done)
    return (index.astype(jnp.float32) + 0.5) * (1.0 / (SPAT << done)) - 0.5


def width(e, done):
    return float(GRID // (FREQ[e] * COUNT[e]) * (1 << done))


def middle(e, high, coord, done):
    index = high * (COUNT[e] >> done) + (coord >> done)
    return (index.astype(jnp.float32) + 0.5) * width(e, done) - 0.5 * GRID


def wave(position):
    y = -position
    t = y * y
    first = y * (3.14159265 + t * (-5.16771278 + t * (2.55016404 + t * (-0.599264529 + t * (0.0821458866 - t * 0.00737043)))))
    double = first * first
    return 1.0, first, 2.0 * double - 1.0, first * (4.0 * double - 3.0)


def speed(modes, px, py):
    wx, wy = wave(px), wave(py)
    total = None
    for j in range(MODES):
        row = modes[j, 0] + modes[j, 1] * wy[1]
        for k in range(2, MODES):
            row = row + modes[j, k] * wy[k]
        row = row * wx[j] if j else row
        total = row if total is None else total + row
    return total + 0.3


def coords():
    sx, sy = lax.axis_index("sx"), lax.axis_index("sy")
    return sx >> 3, (sx >> 1) & 3, (sy >> 1) * 2 + (sx & 1), sy & 1


def device(x, y, z, c):
    return ((x * 4 + y) * 2 + (z & 1), (z >> 1) * 2 + c)


def slot_of(z):
    return (z & 1) * 4 + (z >> 1)


def kernel(w_ref, modes, out_ref, packed, first, both, work, swapped, ready, last, table, final,
           a_send, a_recv, c_send, c_recv, x_send, x_recv, o_send, o_recv):
    x, y, z, c = coords()
    lane = lax.broadcasted_iota(jnp.int32, TILE, 1)
    sub = lax.broadcasted_iota(jnp.int32, TILE, 0)
    low = lane < 64
    half_turn = functools.partial(pltpu.roll, shift=64, axis=1)

    barrier = pltpu.get_barrier_semaphore()

    for d in sorted(range(1, 32), key=lambda d: -min(d & 7, 8 - (d & 7)) - min(d >> 3, 4 - (d >> 3))):
        to = device(x, (y + (d >> 3)) & 3, (z + d) & 7, c)
        pl.semaphore_signal(barrier, inc=1, device_id=to, device_id_type=MESH)

    for d in range(1, 4):
        pl.semaphore_signal(barrier, inc=1, device_id=device((x + d) & 3, y, z, c), device_id_type=MESH)
    pl.semaphore_signal(barrier, inc=1, device_id=device(x, y, z, 1 - c), device_id_type=MESH)

    @pl.loop(0, 32)
    def _(k):
        for jt in range(4):
            re, im = w_ref[0, k, jt], w_ref[1, k, jt]
            packed[0, k, jt * 8 : jt * 8 + 8] = jnp.where(low, re, half_turn(im))
            packed[1, k, jt * 8 : jt * 8 + 8] = jnp.where(low, half_turn(re), im)

    pl.semaphore_wait(barrier, 35)

    me = y * 8 + slot_of(z)

    def first_copy(q, d):
        ty, tz = (y + (d >> 3)) & 3, (z + d) & 7
        return pltpu.make_async_remote_copy(
            src_ref=packed.at[q, :, ty * 8 + tz],
            dst_ref=first.at[q, :, me],
            send_sem=a_send.at[q, d],
            recv_sem=a_recv.at[q, me],
            device_id=device(x, ty, tz, c),
            device_id_type=MESH,
        )

    def first_start(q, begin, count):
        for d in range(count):
            first_copy(q, begin + d).start()

    def first_own(q):
        pltpu.make_async_copy(packed.at[q, :, y * 8 + z], first.at[q, :, me], a_recv.at[q, me]).start()

    def first_sent(q):
        @pl.loop(1, 32)
        def _(d):
            first_copy(q, d).wait_send()

    first_start(0, 1, 31)
    first_start(1, 1, 31)
    first_own(0)
    first_own(1)

    def first_wait(q):
        @pl.loop(0, 32)
        def _(s):
            pltpu.make_async_copy(first.at[q, :, s], first.at[q, :, s], a_recv.at[q, s]).wait()

    def group_of(to):
        return (((to >> 1) + y) & 1) * 2 + ((to + z) & 1)

    mine = group_of(x)

    def position(phase, tile):
        zh = sub & 3
        if phase == 0:
            return x * 8 + (lane >> 6) * 4 + tile * 2 + (sub >> 2), zh * 2 + c
        return tile * 16 + (sub >> 2) * 8 + (lane >> 6) * 4 + mine, zh * 2 + c

    high = ((lane >> 4) & 3, lane & 15)
    chunk = y * 8 + z
    starts = [(chunk // 4, chunk % 4 * 2 + q) for q in range(2)]

    def spot(phase, tile, q, done):
        at = position(phase, tile)
        return [place(starts[q][e], at[e], done[e]) for e in range(2)]

    def make_table(n):
        e, dx, dy = LEVELS[n]
        done = (dx, dy)
        after = (dx + 1, dy) if e == 0 else (dx, dy + 1)
        phase = 0 if n < 6 else 1
        exact = n == 0
        h = [0.5 * width(i, done[i]) for i in range(2)]
        wide = n in (0, 1, 6)
        factor, inner, outer, base = {}, {}, {}, {}
        for tile in range(2):
            at = position(phase, tile)
            for q in range(2):
                new = spot(phase, tile, q, after)
                sp_new = speed(modes, *new)
                base[q, tile] = (new, sp_new)
                if n == 0:
                    factor[q, tile] = sp_new
                    outer[q, tile] = new[0] * h[0]
                    inner[q, tile] = new[1] * h[1]
                else:
                    old = spot(phase, tile, q, done)
                    factor[q, tile] = sp_new - speed(modes, *old)
                    outer[q, tile] = (new[e] - old[e]) * h[e]
        other = 1 - e
        for child in range(2):
            freq = {}
            for tile in range(2 if wide else 1):
                at = list(position(phase, tile))
                parent = [middle(i, high[i], at[i], after[i]) for i in range(2)]
                at[e] = ((at[e] >> (done[e] + 1)) * 2 + child) << done[e]
                mid = [middle(i, high[i], at[i], done[i]) for i in range(2)]
                square = 1.0 + mid[0] * mid[0] + mid[1] * mid[1]
                root = jnp.sqrt(square)
                root_parent = jnp.sqrt(1.0 + parent[0] * parent[0] + parent[1] * parent[1])
                v = (child - 0.5) * 2.0 * h[e]
                step = v * (v + 2.0 * parent[e]) / (root + root_parent)
                freq[tile] = (mid, square, root, v, step)
            constant = {}
            for tile in range(2):
                mid, square, root, v, step = freq[tile if wide else 0]
                for q in range(2):
                    new, sp_new = base[q, tile]
                    constant[q, tile] = frac(new[e] * v) + frac(sp_new * step)

            @pl.loop(0, CHEB[e])
            def _(ko):
                zo = node(e, ko)
                uo = zo * h[e]
                shift = {key: constant[key] + outer[key] * zo for key in constant}
                first_part = {t: uo * (uo + 2.0 * freq[t][0][e]) for t in freq}
                for ki in range(CHEB[other]):
                    ui = float(NODES[other][ki]) * h[other]
                    delta = {}
                    for t in freq:
                        mid, square, root = freq[t][:3]
                        total = first_part[t] + ui * (ui + 2.0 * mid[other])
                        near = square + total
                        if exact:
                            delta[t] = total / (jnp.sqrt(near) + root)
                        else:
                            delta[t] = total * pl.reciprocal(near * lax.rsqrt(near) + root, approx=True)
                    for tile in range(2):
                        for q in range(2):
                            angle = delta[tile if wide else 0] * factor[q, tile] + shift[q, tile]
                            if n == 0:
                                angle = angle + inner[q, tile] * float(NODES[other][ki])
                            cos, sin = turn(angle)
                            k = (ko, ki) if e == 0 else (ki, ko)
                            table[n, q, tile, child, k[0], k[1], 0] = cos
                            table[n, q, tile, child, k[0], k[1], 1] = sin

    def make_final():
        done = (5, 3)
        h = [0.5 * width(i, done[i]) for i in range(2)]
        at = position(1, 0)
        mid = [middle(i, high[i], at[i], done[i]) for i in range(2)]
        square = 1.0 + mid[0] * mid[0] + mid[1] * mid[1]
        root = jnp.sqrt(square)
        here = {}
        for tile in range(2):
            for q in range(2):
                px, py = spot(1, tile, q, done)
                here[q, tile] = (px * h[0], py * h[1], speed(modes, px, py))

        @pl.loop(0, CHEB[0])
        def _(ko):
            zo = node(0, ko)
            uo = zo * h[0]
            shift = {key: frac(here[key][0] * zo) for key in here}
            first_part = uo * (uo + 2.0 * mid[0])
            for ki in range(CHEB[1]):
                zi = float(NODES[1][ki])
                ui = zi * h[1]
                total = first_part + ui * (ui + 2.0 * mid[1])
                delta = total / (jnp.sqrt(square + total) + root)
                for tile in range(2):
                    for q in range(2):
                        angle = shift[q, tile] + frac(here[q, tile][1] * zi) + frac(here[q, tile][2] * delta)
                        cos, sin = turn(angle)
                        final[q, tile, ko, ki, 0] = cos
                        final[q, tile, ko, ki, 1] = sin

    def children(how, own):
        if how == "tile":
            return [(own[0], own[1])] * 2
        axis, bit, size = how
        bit_set = ((sub if axis == 0 else lane) & bit) != 0
        result = []
        for value in own:
            up = pltpu.roll(value, bit, axis)
            down = up if 2 * bit == size else pltpu.roll(value, size - bit, axis)
            result.append((jnp.where(bit_set, up, value), jnp.where(bit_set, value, down)))
        return result

    def level(n, q, how, read, write, begin=0, count=None):
        e = LEVELS[n][0]
        size = CHEB[e]

        @pl.loop(0, CHEB[1 - e] if count is None else count)
        def _(step):
            ko = begin + step
            at = [(k, ko) if e == 0 else (ko, k) for k in range(size)]
            sums = {}
            values = [read(*k) for k in at]
            for tile in range(2):
                parts = [[[], []], [[], []]]
                for i, k in enumerate(at):
                    if how is None:
                        pair_re, pair_im = values[i][tile]
                    else:
                        pair_re = children(how, values[i][0])[tile] if how == "tile" else children(how, [values[i][0][tile]])[0]
                        pair_im = children(how, values[i][1])[tile] if how == "tile" else children(how, [values[i][1][tile]])[0]
                    for child in range(2):
                        cos = table[n, q, tile, child, k[0], k[1], 0]
                        sin = table[n, q, tile, child, k[0], k[1], 1]
                        re, im = pair_re[child], pair_im[child]
                        parts[child][0].append(cos * re - sin * im)
                        parts[child][1].append(sin * re + cos * im)
                sums[tile] = [merge(size, parts[0][r], parts[1][r]) for r in range(2)]
            for tile in range(2):
                for i, k in enumerate(at):
                    write(k[0], k[1], tile, sums[tile][0][i], sums[tile][1][i])

    def read_first(q):
        def read(k0, k1):
            blocks = [first[q, k0 * 8 + k1, t * 8 : t * 8 + 8] for t in range(4)]
            turned = [half_turn(b) for b in blocks]
            re = [jnp.where(low, blocks[t], turned[2 + t]) for t in range(2)]
            im = [jnp.where(low, turned[t], blocks[2 + t]) for t in range(2)]
            return re, im

        return read

    def reader(ref, q):
        return lambda k0, k1: [[ref[q, r, k0, k1, t] for t in range(2)] for r in range(2)]

    def writer(ref, q):
        def write(k0, k1, tile, re, im):
            ref[q, 0, k0, k1, tile] = re
            ref[q, 1, k0, k1, tile] = im

        return write

    def write_both(q):
        def write(k0, k1, tile, re, im):
            both[q, c, 0, k0, k1, tile] = re
            both[q, c, 1, k0, k1, tile] = im

        return write

    def read_both(q):
        def read(k0, k1):
            return [[[both[q, child, r, k0, k1, t] for child in range(2)] for r in range(2)] for t in range(2)]

        return read

    def write_ready(q):
        def write(k0, k1, tile, re, im):
            cos, sin = final[q, tile, k0, k1, 0], final[q, tile, k0, k1, 1]
            re, im = cos * re + sin * im, cos * im - sin * re
            ready[q, 0, k1 * 4 + k0, tile * 8 : tile * 8 + 8] = jnp.where(low, re, half_turn(im))
            ready[q, 1, k1 * 4 + k0, tile * 8 : tile * 8 + 8] = jnp.where(low, half_turn(re), im)

        return write

    def core_copy(q):
        return pltpu.make_async_remote_copy(
            src_ref=both.at[q, c],
            dst_ref=both.at[q, c],
            send_sem=c_send.at[q],
            recv_sem=c_recv.at[q],
            device_id=device(x, y, z, 1 - c),
            device_id_type=MESH,
        )

    def group(q, g, i):
        return work.at[q, :, :, pl.ds(2 * i, 2), g >> 1, pl.ds((g & 1) * 4, 4)]

    def arrived(q, g, i):
        return swapped.at[q, :, :, pl.ds(2 * i, 2), g >> 1, pl.ds((g & 1) * 4, 4)]

    def x_copy(q, d, i):
        t = (x + d) & 3
        return pltpu.make_async_remote_copy(
            src_ref=group(q, group_of(t), i),
            dst_ref=arrived(q, x, i),
            send_sem=x_send.at[q, d, i],
            recv_sem=x_recv.at[q, x, i],
            device_id=device(t, y, z, c),
            device_id_type=MESH,
        )

    def x_wait(q, i):
        for g in range(4):
            part = arrived(q, g, i)
            pltpu.make_async_copy(part, part, x_recv.at[q, g, i]).wait()

    PARTS = ((0, 0, 32), (1, 0, 16), (1, 16, 16))

    def last_copy(part, d):
        q, row, count = PARTS[part]
        rows = pl.ds(row, count)
        tx, ty1, tz1 = (x + (d >> 3)) & 3, ((y >> 1) + (d >> 2)) & 1, ((z >> 1) + d) & 3
        to = device(tx, ty1 * 2 + (mine >> 1), tz1 * 2 + (mine & 1), c)
        return ready.at[q, ty1, rows, tx * 4 + tz1], to

    def landing(part, slot):
        q, row, count = PARTS[part]
        return last.at[q, pl.ds(row, count), slot]

    def last_remote(part, d):
        src, to = last_copy(part, d)
        return pltpu.make_async_remote_copy(
            src_ref=src,
            dst_ref=landing(part, chunk),
            send_sem=o_send.at[part, d],
            recv_sem=o_recv.at[part, chunk],
            device_id=to,
            device_id_type=MESH,
        )

    def start_last(part):
        for d in range(1, 32):
            last_remote(part, d).start()

        @pl.when(x != 0)
        def _():
            last_remote(part, 0).start()

        @pl.when(x == 0)
        def _():
            pltpu.make_async_copy(last_copy(part, 0)[0], landing(part, chunk), o_recv.at[part, chunk]).start()

    def wait_last_sends(part):
        @pl.loop(1, 32)
        def _(d):
            last_remote(part, d).wait_send()

        @pl.when(x != 0)
        def _():
            last_remote(part, 0).wait_send()

    def wait_last(part):
        @pl.loop(0, 32)
        def _(s):
            pltpu.make_async_copy(landing(part, s), landing(part, s), o_recv.at[part, s]).wait()

    z0, z1, z2, y1 = (0, 4, 8), (0, 1, 8), (0, 2, 8), (1, 64, 128)

    def open_half(q):
        first_wait(q)
        level(0, q, z0, read_first(q), write_both(q))
        core_copy(q).start()

    def middle_half(q):
        core_copy(q).wait()
        level(1, q, None, read_both(q), writer(work, q))
        level(2, q, "tile", reader(work, q), writer(work, q))
        level(3, q, z1, reader(work, q), writer(work, q))
        level(4, q, y1, reader(work, q), writer(work, q))

    def swap_half(q):
        level(5, q, z2, reader(work, q), writer(work, q))
        for i in range(4):
            for d in (2, 1, 3):
                x_copy(q, d, i).start()
            pltpu.make_async_copy(group(q, mine, i), arrived(q, x, i), x_recv.at[q, x, i]).start()

    def second_half(q, begin, end):
        @pl.loop(begin, end)
        def _(i):
            x_wait(q, i)
            level(6, q, z0, reader(swapped, q), writer(swapped, q), 2 * i, 2)
            level(7, q, "tile", reader(swapped, q), write_ready(q), 2 * i, 2)

    for n in range(8):
        make_table(n)
    make_final()
    open_half(0)
    middle_half(0)
    swap_half(0)
    open_half(1)
    second_half(0, 0, 4)
    middle_half(1)
    swap_half(1)
    start_last(0)
    second_half(1, 0, 2)
    start_last(1)
    second_half(1, 2, 4)
    start_last(2)

    for part in range(3):
        wait_last(part)

    @pl.loop(0, 8)
    def _(k1):
        for k0 in range(4):
            for jt in range(4):
                zero, one = last[0, k1 * 4 + k0, jt * 8 : jt * 8 + 8], last[1, k1 * 4 + k0, jt * 8 : jt * 8 + 8]
                out_ref[0, k0 * 8 + k1, jt] = jnp.where(low, zero, half_turn(one))
                out_ref[1, k0 * 8 + k1, jt] = jnp.where(low, half_turn(zero), one)

    for q in range(2):
        first_sent(q)
        for d in range(1, 4):
            for i in range(4):
                x_copy(q, d, i).wait_send()
    for part in range(3):
        wait_last_sends(part)


def body(weights_in, speed_modes):
    half = (2, 2, 4, 8, 2, *TILE)
    f32 = jnp.float32
    out = pl.pallas_call(
        kernel,
        out_shape=jax.ShapeDtypeStruct((2, 32, 4, *TILE), f32),
        in_specs=[pl.BlockSpec(memory_space=pltpu.VMEM), pl.BlockSpec(memory_space=pltpu.SMEM)],
        out_specs=pl.BlockSpec(memory_space=pltpu.VMEM),
        scratch_shapes=[
            pltpu.VMEM((2, 32, 32, 128), f32),
            pltpu.VMEM((2, 32, 32, 128), f32),
            pltpu.VMEM((2, *half), f32),
            pltpu.VMEM(half, f32),
            pltpu.VMEM(half, f32),
            pltpu.VMEM((2, 2, 32, 16, 128), f32),
            pltpu.VMEM((2, 32, 32, 128), f32),
            pltpu.VMEM((8, 2, 2, 2, 4, 8, 2, *TILE), f32),
            pltpu.VMEM((2, 2, 4, 8, 2, *TILE), f32),
            pltpu.SemaphoreType.DMA((2, 32)),
            pltpu.SemaphoreType.DMA((2, 32)),
            pltpu.SemaphoreType.DMA((2,)),
            pltpu.SemaphoreType.DMA((2,)),
            pltpu.SemaphoreType.DMA((2, 4, 4)),
            pltpu.SemaphoreType.DMA((2, 4, 4)),
            pltpu.SemaphoreType.DMA((3, 32)),
            pltpu.SemaphoreType.DMA((3, 32)),
        ],
        compiler_params=pltpu.CompilerParams(collective_id=0, has_side_effects=True, vmem_limit_bytes=48 << 20),
    )(weights_in.reshape(2, 32, 4, *TILE), speed_modes)
    return out.reshape(weights_in.shape)


def solution(mesh):
    placed = P(None, None, "sx", "sy", None)
    return jax.shard_map(body, mesh=mesh, in_specs=(placed, P()), out_specs=placed, check_vma=False)
```

```python
import functools

import jax
import jax.numpy as jnp
import numpy as np
from jax import lax
from jax.experimental import pallas as pl
from jax.experimental.pallas import tpu as pltpu
from jax.sharding import PartitionSpec as P

MESH = pl.DeviceIdType.MESH
GRID = 8192
CHEB = (4, 8)
SPAT = 8
FREQ = (4, 16)
COUNT = (32, 8)
MODES = 4
TILE = (8, 128)
LEVELS = ((0, 0, 0), (1, 1, 0), (0, 1, 1), (1, 2, 1), (0, 2, 2), (1, 3, 2), (0, 3, 3), (0, 4, 3))
SIN_POLY = (4.44288292, -7.30824569, 3.60635422, -0.84611165, 0.10982452)
COS_POLY = (1.4142135, -6.97885095, 5.73946038, -1.88355791, 0.31068803)


def cheb_nodes(q):
    return np.cos((2.0 * np.arange(q) + 1.0) * np.pi / (2.0 * q))


NODES = tuple(np.asarray(cheb_nodes(q), np.float32).astype(np.float64) for q in CHEB)


def child_table(q):
    z = cheb_nodes(q)
    points = -0.5 + 0.5 * z
    table = np.ones((q, q))
    for k in range(q):
        for j in range(q):
            if j != k:
                table[k, :] *= (points - z[j]) / (z[k] - z[j])
    return table


def halves(q):
    table = child_table(q)
    even = 0.5 * (table + table[::-1])[: q // 2]
    odd = 0.5 * (table - table[::-1])[: q // 2]
    return even, odd


HALVES = tuple(halves(q) for q in CHEB)


def merge(q, a, b):
    even, odd = HALVES[0 if q == 4 else 1]
    plus = [a[k] + b[q - 1 - k] for k in range(q)]
    minus = [a[k] - b[q - 1 - k] for k in range(q)]
    out = [None] * q
    for k in range(q // 2):
        e = plus[0] * float(even[k, 0])
        o = minus[0] * float(odd[k, 0])
        for j in range(1, q):
            e = e + plus[j] * float(even[k, j])
            o = o + minus[j] * float(odd[k, j])
        out[k] = e + o
        out[q - 1 - k] = e - o
    return out


def frac(v):
    return v - jnp.round(v)


def poly(coefficients, t):
    result = t * coefficients[-1] + coefficients[-2]
    for value in coefficients[-3::-1]:
        result = result * t + value
    return result


def turn(angle):
    r = frac(angle)
    t = r * r
    s = poly(SIN_POLY, t) * r
    c = poly(COS_POLY, t)
    return 1.0 - s * s, s * c


def node(e, k):
    value = jnp.float32(NODES[e][0])
    for i in range(1, CHEB[e]):
        value = jnp.where(k == i, jnp.float32(NODES[e][i]), value)
    return value


def rev(v, bits):
    result = jnp.int32(0)
    for t in range(bits):
        result = result + ((v >> t) & 1) * (1 << (bits - 1 - t))
    return result


def place(start, coord, done):
    index = start * (1 << done) + rev(coord, done)
    return (index.astype(jnp.float32) + 0.5) * (1.0 / (SPAT << done)) - 0.5


def width(e, done):
    return float(GRID // (FREQ[e] * COUNT[e]) * (1 << done))


def middle(e, high, coord, done):
    index = high * (COUNT[e] >> done) + (coord >> done)
    return (index.astype(jnp.float32) + 0.5) * width(e, done) - 0.5 * GRID


def wave(position):
    y = -position
    t = y * y
    first = y * (3.14159265 + t * (-5.16771278 + t * (2.55016404 + t * (-0.599264529 + t * (0.0821458866 - t * 0.00737043)))))
    double = first * first
    return 1.0, first, 2.0 * double - 1.0, first * (4.0 * double - 3.0)


def speed(modes, px, py):
    wx, wy = wave(px), wave(py)
    total = None
    for j in range(MODES):
        row = modes[j, 0] + modes[j, 1] * wy[1]
        for k in range(2, MODES):
            row = row + modes[j, k] * wy[k]
        row = row * wx[j] if j else row
        total = row if total is None else total + row
    return total + 0.3


def coords():
    sx, sy = lax.axis_index("sx"), lax.axis_index("sy")
    return sx >> 3, (sx >> 1) & 3, (sy >> 1) * 2 + (sx & 1), sy & 1


def device(x, y, z, c):
    return ((x * 4 + y) * 2 + (z & 1), (z >> 1) * 2 + c)


def slot_of(z):
    return (z & 1) * 4 + (z >> 1)


def kernel(w_ref, modes, out_ref, packed, first, both, work, swapped, ready, last, table, final,
           a_send, a_recv, c_send, c_recv, x_send, x_recv, o_send, o_recv):
    x, y, z, c = coords()
    lane = lax.broadcasted_iota(jnp.int32, TILE, 1)
    sub = lax.broadcasted_iota(jnp.int32, TILE, 0)
    low = lane < 64
    half_turn = functools.partial(pltpu.roll, shift=64, axis=1)

    barrier = pltpu.get_barrier_semaphore()

    for d in sorted(range(1, 32), key=lambda d: -min(d & 7, 8 - (d & 7)) - min(d >> 3, 4 - (d >> 3))):
        to = device(x, (y + (d >> 3)) & 3, (z + d) & 7, c)
        pl.semaphore_signal(barrier, inc=1, device_id=to, device_id_type=MESH)

    for d in range(1, 4):
        pl.semaphore_signal(barrier, inc=1, device_id=device((x + d) & 3, y, z, c), device_id_type=MESH)
    pl.semaphore_signal(barrier, inc=1, device_id=device(x, y, z, 1 - c), device_id_type=MESH)

    @pl.loop(0, 32)
    def _(k):
        for jt in range(4):
            re, im = w_ref[0, k, jt], w_ref[1, k, jt]
            packed[0, k, jt * 8 : jt * 8 + 8] = jnp.where(low, re, half_turn(im))
            packed[1, k, jt * 8 : jt * 8 + 8] = jnp.where(low, half_turn(re), im)

    pl.semaphore_wait(barrier, 35)

    me = y * 8 + slot_of(z)

    def first_copy(q, d):
        ty, tz = (y + (d >> 3)) & 3, (z + d) & 7
        return pltpu.make_async_remote_copy(
            src_ref=packed.at[q, :, ty * 8 + tz],
            dst_ref=first.at[q, :, me],
            send_sem=a_send.at[q, d],
            recv_sem=a_recv.at[q, me],
            device_id=device(x, ty, tz, c),
            device_id_type=MESH,
        )

    def first_start(q, begin, count):
        for d in range(count):
            first_copy(q, begin + d).start()

    def first_own(q):
        pltpu.make_async_copy(packed.at[q, :, y * 8 + z], first.at[q, :, me], a_recv.at[q, me]).start()

    def first_sent(q):
        @pl.loop(1, 32)
        def _(d):
            first_copy(q, d).wait_send()

    first_start(0, 1, 31)
    first_start(1, 1, 31)
    first_own(0)
    first_own(1)

    def first_wait(q):
        @pl.loop(0, 32)
        def _(s):
            pltpu.make_async_copy(first.at[q, :, s], first.at[q, :, s], a_recv.at[q, s]).wait()

    def group_of(to):
        return (((to >> 1) + y) & 1) * 2 + ((to + z) & 1)

    mine = group_of(x)

    def position(phase, tile):
        zh = sub & 3
        if phase == 0:
            return x * 8 + (lane >> 6) * 4 + tile * 2 + (sub >> 2), zh * 2 + c
        return tile * 16 + (sub >> 2) * 8 + (lane >> 6) * 4 + mine, zh * 2 + c

    high = ((lane >> 4) & 3, lane & 15)
    chunk = y * 8 + z
    starts = [(chunk // 4, chunk % 4 * 2 + q) for q in range(2)]

    def spot(phase, tile, q, done):
        at = position(phase, tile)
        return [place(starts[q][e], at[e], done[e]) for e in range(2)]

    def make_table(n):
        e, dx, dy = LEVELS[n]
        done = (dx, dy)
        after = (dx + 1, dy) if e == 0 else (dx, dy + 1)
        phase = 0 if n < 6 else 1
        exact = n == 0
        h = [0.5 * width(i, done[i]) for i in range(2)]
        wide = n in (0, 1, 6)
        factor, inner, outer, base = {}, {}, {}, {}
        for tile in range(2):
            at = position(phase, tile)
            for q in range(2):
                new = spot(phase, tile, q, after)
                sp_new = speed(modes, *new)
                base[q, tile] = (new, sp_new)
                if n == 0:
                    factor[q, tile] = sp_new
                    outer[q, tile] = new[0] * h[0]
                    inner[q, tile] = new[1] * h[1]
                else:
                    old = spot(phase, tile, q, done)
                    factor[q, tile] = sp_new - speed(modes, *old)
                    outer[q, tile] = (new[e] - old[e]) * h[e]
        other = 1 - e
        for child in range(2):
            freq = {}
            for tile in range(2 if wide else 1):
                at = list(position(phase, tile))
                parent = [middle(i, high[i], at[i], after[i]) for i in range(2)]
                at[e] = ((at[e] >> (done[e] + 1)) * 2 + child) << done[e]
                mid = [middle(i, high[i], at[i], done[i]) for i in range(2)]
                square = 1.0 + mid[0] * mid[0] + mid[1] * mid[1]
                root = jnp.sqrt(square)
                root_parent = jnp.sqrt(1.0 + parent[0] * parent[0] + parent[1] * parent[1])
                v = (child - 0.5) * 2.0 * h[e]
                step = v * (v + 2.0 * parent[e]) / (root + root_parent)
                freq[tile] = (mid, square, root, v, step)
            constant = {}
            for tile in range(2):
                mid, square, root, v, step = freq[tile if wide else 0]
                for q in range(2):
                    new, sp_new = base[q, tile]
                    constant[q, tile] = frac(new[e] * v) + frac(sp_new * step)

            @pl.loop(0, CHEB[e])
            def _(ko):
                zo = node(e, ko)
                uo = zo * h[e]
                shift = {key: constant[key] + outer[key] * zo for key in constant}
                first_part = {t: uo * (uo + 2.0 * freq[t][0][e]) for t in freq}
                for ki in range(CHEB[other]):
                    ui = float(NODES[other][ki]) * h[other]
                    delta = {}
                    for t in freq:
                        mid, square, root = freq[t][:3]
                        total = first_part[t] + ui * (ui + 2.0 * mid[other])
                        near = square + total
                        if exact:
                            delta[t] = total / (jnp.sqrt(near) + root)
                        else:
                            delta[t] = total * pl.reciprocal(near * lax.rsqrt(near) + root, approx=True)
                    for tile in range(2):
                        for q in range(2):
                            angle = delta[tile if wide else 0] * factor[q, tile] + shift[q, tile]
                            if n == 0:
                                angle = angle + inner[q, tile] * float(NODES[other][ki])
                            cos, sin = turn(angle)
                            k = (ko, ki) if e == 0 else (ki, ko)
                            table[n, q, tile, child, k[0], k[1], 0] = cos
                            table[n, q, tile, child, k[0], k[1], 1] = sin

    def make_final():
        done = (5, 3)
        h = [0.5 * width(i, done[i]) for i in range(2)]
        at = position(1, 0)
        mid = [middle(i, high[i], at[i], done[i]) for i in range(2)]
        square = 1.0 + mid[0] * mid[0] + mid[1] * mid[1]
        root = jnp.sqrt(square)
        here = {}
        for tile in range(2):
            for q in range(2):
                px, py = spot(1, tile, q, done)
                here[q, tile] = (px * h[0], py * h[1], speed(modes, px, py))

        @pl.loop(0, CHEB[0])
        def _(ko):
            zo = node(0, ko)
            uo = zo * h[0]
            shift = {key: frac(here[key][0] * zo) for key in here}
            first_part = uo * (uo + 2.0 * mid[0])
            for ki in range(CHEB[1]):
                zi = float(NODES[1][ki])
                ui = zi * h[1]
                total = first_part + ui * (ui + 2.0 * mid[1])
                delta = total / (jnp.sqrt(square + total) + root)
                for tile in range(2):
                    for q in range(2):
                        angle = shift[q, tile] + frac(here[q, tile][1] * zi) + frac(here[q, tile][2] * delta)
                        cos, sin = turn(angle)
                        final[q, tile, ko, ki, 0] = cos
                        final[q, tile, ko, ki, 1] = sin

    def children(how, own):
        if how == "tile":
            return [(own[0], own[1])] * 2
        axis, bit, size = how
        bit_set = ((sub if axis == 0 else lane) & bit) != 0
        result = []
        for value in own:
            up = pltpu.roll(value, bit, axis)
            down = up if 2 * bit == size else pltpu.roll(value, size - bit, axis)
            result.append((jnp.where(bit_set, up, value), jnp.where(bit_set, value, down)))
        return result

    def level(n, q, how, read, write, begin=0, count=None):
        e = LEVELS[n][0]
        size = CHEB[e]

        @pl.loop(0, CHEB[1 - e] if count is None else count)
        def _(step):
            ko = begin + step
            at = [(k, ko) if e == 0 else (ko, k) for k in range(size)]
            sums = {}
            values = [read(*k) for k in at]
            for tile in range(2):
                parts = [[[], []], [[], []]]
                for i, k in enumerate(at):
                    if how is None:
                        pair_re, pair_im = values[i][tile]
                    else:
                        pair_re = children(how, values[i][0])[tile] if how == "tile" else children(how, [values[i][0][tile]])[0]
                        pair_im = children(how, values[i][1])[tile] if how == "tile" else children(how, [values[i][1][tile]])[0]
                    for child in range(2):
                        cos = table[n, q, tile, child, k[0], k[1], 0]
                        sin = table[n, q, tile, child, k[0], k[1], 1]
                        re, im = pair_re[child], pair_im[child]
                        parts[child][0].append(cos * re - sin * im)
                        parts[child][1].append(sin * re + cos * im)
                sums[tile] = [merge(size, parts[0][r], parts[1][r]) for r in range(2)]
            for tile in range(2):
                for i, k in enumerate(at):
                    write(k[0], k[1], tile, sums[tile][0][i], sums[tile][1][i])

    def read_first(q):
        def read(k0, k1):
            blocks = [first[q, k0 * 8 + k1, t * 8 : t * 8 + 8] for t in range(4)]
            turned = [half_turn(b) for b in blocks]
            re = [jnp.where(low, blocks[t], turned[2 + t]) for t in range(2)]
            im = [jnp.where(low, turned[t], blocks[2 + t]) for t in range(2)]
            return re, im

        return read

    def reader(ref, q):
        return lambda k0, k1: [[ref[q, r, k0, k1, t] for t in range(2)] for r in range(2)]

    def writer(ref, q):
        def write(k0, k1, tile, re, im):
            ref[q, 0, k0, k1, tile] = re
            ref[q, 1, k0, k1, tile] = im

        return write

    def write_both(q):
        def write(k0, k1, tile, re, im):
            both[q, c, 0, k0, k1, tile] = re
            both[q, c, 1, k0, k1, tile] = im

        return write

    def read_both(q):
        def read(k0, k1):
            return [[[both[q, child, r, k0, k1, t] for child in range(2)] for r in range(2)] for t in range(2)]

        return read

    def write_ready(q):
        def write(k0, k1, tile, re, im):
            cos, sin = final[q, tile, k0, k1, 0], final[q, tile, k0, k1, 1]
            re, im = cos * re + sin * im, cos * im - sin * re
            ready[q, 0, k1 * 4 + k0, tile * 8 : tile * 8 + 8] = jnp.where(low, re, half_turn(im))
            ready[q, 1, k1 * 4 + k0, tile * 8 : tile * 8 + 8] = jnp.where(low, half_turn(re), im)

        return write

    def core_copy(q):
        return pltpu.make_async_remote_copy(
            src_ref=both.at[q, c],
            dst_ref=both.at[q, c],
            send_sem=c_send.at[q],
            recv_sem=c_recv.at[q],
            device_id=device(x, y, z, 1 - c),
            device_id_type=MESH,
        )

    def group(q, g, i):
        return work.at[q, :, :, pl.ds(2 * i, 2), g >> 1, pl.ds((g & 1) * 4, 4)]

    def arrived(q, g, i):
        return swapped.at[q, :, :, pl.ds(2 * i, 2), g >> 1, pl.ds((g & 1) * 4, 4)]

    def x_copy(q, d, i):
        t = (x + d) & 3
        return pltpu.make_async_remote_copy(
            src_ref=group(q, group_of(t), i),
            dst_ref=arrived(q, x, i),
            send_sem=x_send.at[q, d, i],
            recv_sem=x_recv.at[q, x, i],
            device_id=device(t, y, z, c),
            device_id_type=MESH,
        )

    def x_wait(q, i):
        for g in range(4):
            part = arrived(q, g, i)
            pltpu.make_async_copy(part, part, x_recv.at[q, g, i]).wait()

    PARTS = ((0, 0, 32), (1, 0, 16), (1, 16, 16))

    def last_copy(part, d):
        q, row, count = PARTS[part]
        rows = pl.ds(row, count)
        tx, ty1, tz1 = (x + (d >> 3)) & 3, ((y >> 1) + (d >> 2)) & 1, ((z >> 1) + d) & 3
        to = device(tx, ty1 * 2 + (mine >> 1), tz1 * 2 + (mine & 1), c)
        return ready.at[q, ty1, rows, tx * 4 + tz1], to

    def landing(part, slot):
        q, row, count = PARTS[part]
        return last.at[q, pl.ds(row, count), slot]

    def last_remote(part, d):
        src, to = last_copy(part, d)
        return pltpu.make_async_remote_copy(
            src_ref=src,
            dst_ref=landing(part, chunk),
            send_sem=o_send.at[part, d],
            recv_sem=o_recv.at[part, chunk],
            device_id=to,
            device_id_type=MESH,
        )

    def start_last(part):
        for d in range(1, 32):
            last_remote(part, d).start()

        @pl.when(x != 0)
        def _():
            last_remote(part, 0).start()

        @pl.when(x == 0)
        def _():
            pltpu.make_async_copy(last_copy(part, 0)[0], landing(part, chunk), o_recv.at[part, chunk]).start()

    def wait_last_sends(part):
        @pl.loop(1, 32)
        def _(d):
            last_remote(part, d).wait_send()

        @pl.when(x != 0)
        def _():
            last_remote(part, 0).wait_send()

    def wait_last(part):
        @pl.loop(0, 32)
        def _(s):
            pltpu.make_async_copy(landing(part, s), landing(part, s), o_recv.at[part, s]).wait()

    z0, z1, z2, y1 = (0, 4, 8), (0, 1, 8), (0, 2, 8), (1, 64, 128)

    def open_half(q):
        first_wait(q)
        level(0, q, z0, read_first(q), write_both(q))
        core_copy(q).start()

    def middle_half(q):
        core_copy(q).wait()
        level(1, q, None, read_both(q), writer(work, q))
        level(2, q, "tile", reader(work, q), writer(work, q))
        level(3, q, z1, reader(work, q), writer(work, q))
        level(4, q, y1, reader(work, q), writer(work, q))

    def swap_half(q):
        level(5, q, z2, reader(work, q), writer(work, q))
        for i in range(4):
            for d in (2, 1, 3):
                x_copy(q, d, i).start()
            pltpu.make_async_copy(group(q, mine, i), arrived(q, x, i), x_recv.at[q, x, i]).start()

    def second_half(q, begin, end):
        @pl.loop(begin, end)
        def _(i):
            x_wait(q, i)
            level(6, q, z0, reader(swapped, q), writer(swapped, q), 2 * i, 2)
            level(7, q, "tile", reader(swapped, q), write_ready(q), 2 * i, 2)

    for n in range(8):
        make_table(n)
    make_final()
    open_half(0)
    middle_half(0)
    swap_half(0)
    open_half(1)
    second_half(0, 0, 4)
    middle_half(1)
    start_last(0)
    swap_half(1)
    second_half(1, 0, 2)
    start_last(1)
    second_half(1, 2, 4)
    start_last(2)

    for part in range(3):
        wait_last(part)

    @pl.loop(0, 8)
    def _(k1):
        for k0 in range(4):
            for jt in range(4):
                zero, one = last[0, k1 * 4 + k0, jt * 8 : jt * 8 + 8], last[1, k1 * 4 + k0, jt * 8 : jt * 8 + 8]
                out_ref[0, k0 * 8 + k1, jt] = jnp.where(low, zero, half_turn(one))
                out_ref[1, k0 * 8 + k1, jt] = jnp.where(low, half_turn(zero), one)

    for q in range(2):
        first_sent(q)
        for d in range(1, 4):
            for i in range(4):
                x_copy(q, d, i).wait_send()
    for part in range(3):
        wait_last_sends(part)


def body(weights_in, speed_modes):
    half = (2, 2, 4, 8, 2, *TILE)
    f32 = jnp.float32
    out = pl.pallas_call(
        kernel,
        out_shape=jax.ShapeDtypeStruct((2, 32, 4, *TILE), f32),
        in_specs=[pl.BlockSpec(memory_space=pltpu.VMEM), pl.BlockSpec(memory_space=pltpu.SMEM)],
        out_specs=pl.BlockSpec(memory_space=pltpu.VMEM),
        scratch_shapes=[
            pltpu.VMEM((2, 32, 32, 128), f32),
            pltpu.VMEM((2, 32, 32, 128), f32),
            pltpu.VMEM((2, *half), f32),
            pltpu.VMEM(half, f32),
            pltpu.VMEM(half, f32),
            pltpu.VMEM((2, 2, 32, 16, 128), f32),
            pltpu.VMEM((2, 32, 32, 128), f32),
            pltpu.VMEM((8, 2, 2, 2, 4, 8, 2, *TILE), f32),
            pltpu.VMEM((2, 2, 4, 8, 2, *TILE), f32),
            pltpu.SemaphoreType.DMA((2, 32)),
            pltpu.SemaphoreType.DMA((2, 32)),
            pltpu.SemaphoreType.DMA((2,)),
            pltpu.SemaphoreType.DMA((2,)),
            pltpu.SemaphoreType.DMA((2, 4, 4)),
            pltpu.SemaphoreType.DMA((2, 4, 4)),
            pltpu.SemaphoreType.DMA((3, 32)),
            pltpu.SemaphoreType.DMA((3, 32)),
        ],
        compiler_params=pltpu.CompilerParams(collective_id=0, has_side_effects=True, vmem_limit_bytes=48 << 20),
    )(weights_in.reshape(2, 32, 4, *TILE), speed_modes)
    return out.reshape(weights_in.shape)


def solution(mesh):
    placed = P(None, None, "sx", "sy", None)
    return jax.shard_map(body, mesh=mesh, in_specs=(placed, P()), out_specs=placed, check_vma=False)
```

```python
import functools

import jax
import jax.numpy as jnp
import numpy as np
from jax import lax
from jax.experimental import pallas as pl
from jax.experimental.pallas import tpu as pltpu
from jax.sharding import PartitionSpec as P

MESH = pl.DeviceIdType.MESH
GRID = 8192
CHEB = (4, 8)
SPAT = 8
FREQ = (4, 16)
COUNT = (32, 8)
MODES = 4
TILE = (8, 128)
LEVELS = ((0, 0, 0), (1, 1, 0), (0, 1, 1), (1, 2, 1), (0, 2, 2), (1, 3, 2), (0, 3, 3), (0, 4, 3))
SIN_POLY = (4.44288292, -7.30824569, 3.60635422, -0.84611165, 0.10982452)
COS_POLY = (1.4142135, -6.97885095, 5.73946038, -1.88355791, 0.31068803)


def cheb_nodes(q):
    return np.cos((2.0 * np.arange(q) + 1.0) * np.pi / (2.0 * q))


NODES = tuple(np.asarray(cheb_nodes(q), np.float32).astype(np.float64) for q in CHEB)


def child_table(q):
    z = cheb_nodes(q)
    points = -0.5 + 0.5 * z
    table = np.ones((q, q))
    for k in range(q):
        for j in range(q):
            if j != k:
                table[k, :] *= (points - z[j]) / (z[k] - z[j])
    return table


def halves(q):
    table = child_table(q)
    even = 0.5 * (table + table[::-1])[: q // 2]
    odd = 0.5 * (table - table[::-1])[: q // 2]
    return even, odd


HALVES = tuple(halves(q) for q in CHEB)


def merge(q, a, b):
    even, odd = HALVES[0 if q == 4 else 1]
    plus = [a[k] + b[q - 1 - k] for k in range(q)]
    minus = [a[k] - b[q - 1 - k] for k in range(q)]
    out = [None] * q
    for k in range(q // 2):
        e = plus[0] * float(even[k, 0])
        o = minus[0] * float(odd[k, 0])
        for j in range(1, q):
            e = e + plus[j] * float(even[k, j])
            o = o + minus[j] * float(odd[k, j])
        out[k] = e + o
        out[q - 1 - k] = e - o
    return out


def frac(v):
    return v - jnp.round(v)


def poly(coefficients, t):
    result = t * coefficients[-1] + coefficients[-2]
    for value in coefficients[-3::-1]:
        result = result * t + value
    return result


def turn(angle):
    r = frac(angle)
    t = r * r
    s = poly(SIN_POLY, t) * r
    c = poly(COS_POLY, t)
    return 1.0 - s * s, s * c


def node(e, k):
    value = jnp.float32(NODES[e][0])
    for i in range(1, CHEB[e]):
        value = jnp.where(k == i, jnp.float32(NODES[e][i]), value)
    return value


def rev(v, bits):
    result = jnp.int32(0)
    for t in range(bits):
        result = result + ((v >> t) & 1) * (1 << (bits - 1 - t))
    return result


def place(start, coord, done):
    index = start * (1 << done) + rev(coord, done)
    return (index.astype(jnp.float32) + 0.5) * (1.0 / (SPAT << done)) - 0.5


def width(e, done):
    return float(GRID // (FREQ[e] * COUNT[e]) * (1 << done))


def middle(e, high, coord, done):
    index = high * (COUNT[e] >> done) + (coord >> done)
    return (index.astype(jnp.float32) + 0.5) * width(e, done) - 0.5 * GRID


def wave(position):
    y = -position
    t = y * y
    first = y * (3.14159265 + t * (-5.16771278 + t * (2.55016404 + t * (-0.599264529 + t * (0.0821458866 - t * 0.00737043)))))
    double = first * first
    return 1.0, first, 2.0 * double - 1.0, first * (4.0 * double - 3.0)


def speed(modes, px, py):
    wx, wy = wave(px), wave(py)
    total = None
    for j in range(MODES):
        row = modes[j, 0] + modes[j, 1] * wy[1]
        for k in range(2, MODES):
            row = row + modes[j, k] * wy[k]
        row = row * wx[j] if j else row
        total = row if total is None else total + row
    return total + 0.3


def coords():
    sx, sy = lax.axis_index("sx"), lax.axis_index("sy")
    return sx >> 3, (sx >> 1) & 3, (sy >> 1) * 2 + (sx & 1), sy & 1


def device(x, y, z, c):
    return ((x * 4 + y) * 2 + (z & 1), (z >> 1) * 2 + c)


def slot_of(z):
    return (z & 1) * 4 + (z >> 1)


def kernel(w_ref, modes, out_ref, packed, first, both, work, swapped, ready, last, table, final,
           a_send, a_recv, c_send, c_recv, x_send, x_recv, o_send, o_recv):
    x, y, z, c = coords()
    lane = lax.broadcasted_iota(jnp.int32, TILE, 1)
    sub = lax.broadcasted_iota(jnp.int32, TILE, 0)
    low = lane < 64
    half_turn = functools.partial(pltpu.roll, shift=64, axis=1)

    barrier = pltpu.get_barrier_semaphore()

    for d in sorted(range(1, 32), key=lambda d: -min(d & 7, 8 - (d & 7)) - min(d >> 3, 4 - (d >> 3))):
        to = device(x, (y + (d >> 3)) & 3, (z + d) & 7, c)
        pl.semaphore_signal(barrier, inc=1, device_id=to, device_id_type=MESH)

    for d in range(1, 4):
        pl.semaphore_signal(barrier, inc=1, device_id=device((x + d) & 3, y, z, c), device_id_type=MESH)
    pl.semaphore_signal(barrier, inc=1, device_id=device(x, y, z, 1 - c), device_id_type=MESH)

    @pl.loop(0, 32)
    def _(k):
        for jt in range(4):
            re, im = w_ref[0, k, jt], w_ref[1, k, jt]
            packed[0, k, jt * 8 : jt * 8 + 8] = jnp.where(low, re, half_turn(im))
            packed[1, k, jt * 8 : jt * 8 + 8] = jnp.where(low, half_turn(re), im)

    pl.semaphore_wait(barrier, 35)

    me = y * 8 + slot_of(z)

    def first_copy(q, d):
        ty, tz = (y + (d >> 3)) & 3, (z + d) & 7
        return pltpu.make_async_remote_copy(
            src_ref=packed.at[q, :, ty * 8 + tz],
            dst_ref=first.at[q, :, me],
            send_sem=a_send.at[q, d],
            recv_sem=a_recv.at[q, me],
            device_id=device(x, ty, tz, c),
            device_id_type=MESH,
        )

    def first_start(q, begin, count):
        for d in range(count):
            first_copy(q, begin + d).start()

    def first_own(q):
        pltpu.make_async_copy(packed.at[q, :, y * 8 + z], first.at[q, :, me], a_recv.at[q, me]).start()

    def first_sent(q):
        @pl.loop(1, 32)
        def _(d):
            first_copy(q, d).wait_send()

    first_start(0, 1, 31)
    first_start(1, 1, 31)
    first_own(0)
    first_own(1)

    def first_wait(q):
        @pl.loop(0, 32)
        def _(s):
            pltpu.make_async_copy(first.at[q, :, s], first.at[q, :, s], a_recv.at[q, s]).wait()

    def group_of(to):
        return (((to >> 1) + y) & 1) * 2 + ((to + z) & 1)

    mine = group_of(x)

    def position(phase, tile):
        zh = sub & 3
        if phase == 0:
            return x * 8 + (lane >> 6) * 4 + tile * 2 + (sub >> 2), zh * 2 + c
        return tile * 16 + (sub >> 2) * 8 + (lane >> 6) * 4 + mine, zh * 2 + c

    high = ((lane >> 4) & 3, lane & 15)
    chunk = y * 8 + z
    starts = [(chunk // 4, chunk % 4 * 2 + q) for q in range(2)]

    def spot(phase, tile, q, done):
        at = position(phase, tile)
        return [place(starts[q][e], at[e], done[e]) for e in range(2)]

    def make_table(n):
        e, dx, dy = LEVELS[n]
        done = (dx, dy)
        after = (dx + 1, dy) if e == 0 else (dx, dy + 1)
        phase = 0 if n < 6 else 1
        exact = n == 0
        h = [0.5 * width(i, done[i]) for i in range(2)]
        wide = n in (0, 1, 6)
        factor, inner, outer, base = {}, {}, {}, {}
        for tile in range(2):
            at = position(phase, tile)
            for q in range(2):
                new = spot(phase, tile, q, after)
                sp_new = speed(modes, *new)
                base[q, tile] = (new, sp_new)
                if n == 0:
                    factor[q, tile] = sp_new
                    outer[q, tile] = new[0] * h[0]
                    inner[q, tile] = new[1] * h[1]
                else:
                    old = spot(phase, tile, q, done)
                    factor[q, tile] = sp_new - speed(modes, *old)
                    outer[q, tile] = (new[e] - old[e]) * h[e]
        other = 1 - e
        for child in range(2):
            freq = {}
            for tile in range(2 if wide else 1):
                at = list(position(phase, tile))
                parent = [middle(i, high[i], at[i], after[i]) for i in range(2)]
                at[e] = ((at[e] >> (done[e] + 1)) * 2 + child) << done[e]
                mid = [middle(i, high[i], at[i], done[i]) for i in range(2)]
                square = 1.0 + mid[0] * mid[0] + mid[1] * mid[1]
                root = jnp.sqrt(square)
                root_parent = jnp.sqrt(1.0 + parent[0] * parent[0] + parent[1] * parent[1])
                v = (child - 0.5) * 2.0 * h[e]
                step = v * (v + 2.0 * parent[e]) / (root + root_parent)
                freq[tile] = (mid, square, root, v, step)
            constant = {}
            for tile in range(2):
                mid, square, root, v, step = freq[tile if wide else 0]
                for q in range(2):
                    new, sp_new = base[q, tile]
                    constant[q, tile] = frac(new[e] * v) + frac(sp_new * step)

            @pl.loop(0, CHEB[e])
            def _(ko):
                zo = node(e, ko)
                uo = zo * h[e]
                shift = {key: constant[key] + outer[key] * zo for key in constant}
                first_part = {t: uo * (uo + 2.0 * freq[t][0][e]) for t in freq}
                for ki in range(CHEB[other]):
                    ui = float(NODES[other][ki]) * h[other]
                    delta = {}
                    for t in freq:
                        mid, square, root = freq[t][:3]
                        total = first_part[t] + ui * (ui + 2.0 * mid[other])
                        near = square + total
                        if exact:
                            delta[t] = total / (jnp.sqrt(near) + root)
                        else:
                            delta[t] = total * pl.reciprocal(near * lax.rsqrt(near) + root, approx=True)
                    for tile in range(2):
                        for q in range(2):
                            angle = delta[tile if wide else 0] * factor[q, tile] + shift[q, tile]
                            if n == 0:
                                angle = angle + inner[q, tile] * float(NODES[other][ki])
                            cos, sin = turn(angle)
                            k = (ko, ki) if e == 0 else (ki, ko)
                            table[n, q, tile, child, k[0], k[1], 0] = cos
                            table[n, q, tile, child, k[0], k[1], 1] = sin

    def make_final():
        done = (5, 3)
        h = [0.5 * width(i, done[i]) for i in range(2)]
        at = position(1, 0)
        mid = [middle(i, high[i], at[i], done[i]) for i in range(2)]
        square = 1.0 + mid[0] * mid[0] + mid[1] * mid[1]
        root = jnp.sqrt(square)
        here = {}
        for tile in range(2):
            for q in range(2):
                px, py = spot(1, tile, q, done)
                here[q, tile] = (px * h[0], py * h[1], speed(modes, px, py))

        @pl.loop(0, CHEB[0])
        def _(ko):
            zo = node(0, ko)
            uo = zo * h[0]
            shift = {key: frac(here[key][0] * zo) for key in here}
            first_part = uo * (uo + 2.0 * mid[0])
            for ki in range(CHEB[1]):
                zi = float(NODES[1][ki])
                ui = zi * h[1]
                total = first_part + ui * (ui + 2.0 * mid[1])
                delta = total / (jnp.sqrt(square + total) + root)
                for tile in range(2):
                    for q in range(2):
                        angle = shift[q, tile] + frac(here[q, tile][1] * zi) + frac(here[q, tile][2] * delta)
                        cos, sin = turn(angle)
                        final[q, tile, ko, ki, 0] = cos
                        final[q, tile, ko, ki, 1] = sin

    def children(how, own):
        if how == "tile":
            return [(own[0], own[1])] * 2
        axis, bit, size = how
        bit_set = ((sub if axis == 0 else lane) & bit) != 0
        result = []
        for value in own:
            up = pltpu.roll(value, bit, axis)
            down = up if 2 * bit == size else pltpu.roll(value, size - bit, axis)
            result.append((jnp.where(bit_set, up, value), jnp.where(bit_set, value, down)))
        return result

    def level(n, q, how, read, write, begin=0, count=None):
        e = LEVELS[n][0]
        size = CHEB[e]

        @pl.loop(0, CHEB[1 - e] if count is None else count)
        def _(step):
            ko = begin + step
            at = [(k, ko) if e == 0 else (ko, k) for k in range(size)]
            sums = {}
            values = [read(*k) for k in at]
            for tile in range(2):
                parts = [[[], []], [[], []]]
                for i, k in enumerate(at):
                    if how is None:
                        pair_re, pair_im = values[i][tile]
                    else:
                        pair_re = children(how, values[i][0])[tile] if how == "tile" else children(how, [values[i][0][tile]])[0]
                        pair_im = children(how, values[i][1])[tile] if how == "tile" else children(how, [values[i][1][tile]])[0]
                    for child in range(2):
                        cos = table[n, q, tile, child, k[0], k[1], 0]
                        sin = table[n, q, tile, child, k[0], k[1], 1]
                        re, im = pair_re[child], pair_im[child]
                        parts[child][0].append(cos * re - sin * im)
                        parts[child][1].append(sin * re + cos * im)
                sums[tile] = [merge(size, parts[0][r], parts[1][r]) for r in range(2)]
            for tile in range(2):
                for i, k in enumerate(at):
                    write(k[0], k[1], tile, sums[tile][0][i], sums[tile][1][i])

    def read_first(q):
        def read(k0, k1):
            blocks = [first[q, k0 * 8 + k1, t * 8 : t * 8 + 8] for t in range(4)]
            turned = [half_turn(b) for b in blocks]
            re = [jnp.where(low, blocks[t], turned[2 + t]) for t in range(2)]
            im = [jnp.where(low, turned[t], blocks[2 + t]) for t in range(2)]
            return re, im

        return read

    def reader(ref, q):
        return lambda k0, k1: [[ref[q, r, k0, k1, t] for t in range(2)] for r in range(2)]

    def writer(ref, q):
        def write(k0, k1, tile, re, im):
            ref[q, 0, k0, k1, tile] = re
            ref[q, 1, k0, k1, tile] = im

        return write

    def write_both(q):
        def write(k0, k1, tile, re, im):
            both[q, c, 0, k0, k1, tile] = re
            both[q, c, 1, k0, k1, tile] = im

        return write

    def read_both(q):
        def read(k0, k1):
            return [[[both[q, child, r, k0, k1, t] for child in range(2)] for r in range(2)] for t in range(2)]

        return read

    def write_ready(q):
        def write(k0, k1, tile, re, im):
            cos, sin = final[q, tile, k0, k1, 0], final[q, tile, k0, k1, 1]
            re, im = cos * re + sin * im, cos * im - sin * re
            ready[q, 0, k1 * 4 + k0, tile * 8 : tile * 8 + 8] = jnp.where(low, re, half_turn(im))
            ready[q, 1, k1 * 4 + k0, tile * 8 : tile * 8 + 8] = jnp.where(low, half_turn(re), im)

        return write

    def core_copy(q):
        return pltpu.make_async_remote_copy(
            src_ref=both.at[q, c],
            dst_ref=both.at[q, c],
            send_sem=c_send.at[q],
            recv_sem=c_recv.at[q],
            device_id=device(x, y, z, 1 - c),
            device_id_type=MESH,
        )

    def group(q, g, i):
        return work.at[q, :, :, pl.ds(2 * i, 2), g >> 1, pl.ds((g & 1) * 4, 4)]

    def arrived(q, g, i):
        return swapped.at[q, :, :, pl.ds(2 * i, 2), g >> 1, pl.ds((g & 1) * 4, 4)]

    def x_copy(q, d, i):
        t = (x + d) & 3
        return pltpu.make_async_remote_copy(
            src_ref=group(q, group_of(t), i),
            dst_ref=arrived(q, x, i),
            send_sem=x_send.at[q, d, i],
            recv_sem=x_recv.at[q, x, i],
            device_id=device(t, y, z, c),
            device_id_type=MESH,
        )

    def x_wait(q, i):
        for g in range(4):
            part = arrived(q, g, i)
            pltpu.make_async_copy(part, part, x_recv.at[q, g, i]).wait()

    PARTS = ((0, 0, 32), (1, 0, 16), (1, 16, 16))

    def last_copy(part, d):
        q, row, count = PARTS[part]
        rows = pl.ds(row, count)
        tx, ty1, tz1 = (x + (d >> 3)) & 3, ((y >> 1) + (d >> 2)) & 1, ((z >> 1) + d) & 3
        to = device(tx, ty1 * 2 + (mine >> 1), tz1 * 2 + (mine & 1), c)
        return ready.at[q, ty1, rows, tx * 4 + tz1], to

    def landing(part, slot):
        q, row, count = PARTS[part]
        return last.at[q, pl.ds(row, count), slot]

    def last_remote(part, d):
        src, to = last_copy(part, d)
        return pltpu.make_async_remote_copy(
            src_ref=src,
            dst_ref=landing(part, chunk),
            send_sem=o_send.at[part, d],
            recv_sem=o_recv.at[part, chunk],
            device_id=to,
            device_id_type=MESH,
        )

    def start_last(part):
        for d in range(1, 32):
            last_remote(part, d).start()

        @pl.when(x != 0)
        def _():
            last_remote(part, 0).start()

        @pl.when(x == 0)
        def _():
            pltpu.make_async_copy(last_copy(part, 0)[0], landing(part, chunk), o_recv.at[part, chunk]).start()

    def wait_last_sends(part):
        @pl.loop(1, 32)
        def _(d):
            last_remote(part, d).wait_send()

        @pl.when(x != 0)
        def _():
            last_remote(part, 0).wait_send()

    def wait_last(part):
        @pl.loop(0, 32)
        def _(s):
            pltpu.make_async_copy(landing(part, s), landing(part, s), o_recv.at[part, s]).wait()

    z0, z1, z2, y1 = (0, 4, 8), (0, 1, 8), (0, 2, 8), (1, 64, 128)

    def open_half(q):
        first_wait(q)
        level(0, q, z0, read_first(q), write_both(q))
        core_copy(q).start()

    def middle_half(q):
        core_copy(q).wait()
        level(1, q, None, read_both(q), writer(work, q))
        level(2, q, "tile", reader(work, q), writer(work, q))
        level(3, q, z1, reader(work, q), writer(work, q))
        level(4, q, y1, reader(work, q), writer(work, q))

    def swap_half(q):
        level(5, q, z2, reader(work, q), writer(work, q))
        for i in range(4):
            for d in (2, 1, 3):
                x_copy(q, d, i).start()
            pltpu.make_async_copy(group(q, mine, i), arrived(q, x, i), x_recv.at[q, x, i]).start()

    def second_half(q, begin, end):
        @pl.loop(begin, end)
        def _(i):
            x_wait(q, i)
            level(6, q, z0, reader(swapped, q), writer(swapped, q), 2 * i, 2)
            level(7, q, "tile", reader(swapped, q), write_ready(q), 2 * i, 2)

    for n in range(8):
        make_table(n)
    make_final()
    open_half(0)
    middle_half(0)
    swap_half(0)
    open_half(1)
    second_half(0, 0, 4)
    middle_half(1)
    start_last(0)
    swap_half(1)
    second_half(1, 0, 2)
    start_last(1)
    second_half(1, 2, 4)
    start_last(2)

    wait_last(0)
    for part in (1, 2):
        wait_last(part)

        @pl.loop(part * 4 - 4, part * 4)
        def _(k1):
            for k0 in range(4):
                for jt in range(4):
                    zero, one = last[0, k1 * 4 + k0, jt * 8 : jt * 8 + 8], last[1, k1 * 4 + k0, jt * 8 : jt * 8 + 8]
                    out_ref[0, k0 * 8 + k1, jt] = jnp.where(low, zero, half_turn(one))
                    out_ref[1, k0 * 8 + k1, jt] = jnp.where(low, half_turn(zero), one)

    for q in range(2):
        first_sent(q)
        for d in range(1, 4):
            for i in range(4):
                x_copy(q, d, i).wait_send()
    for part in range(3):
        wait_last_sends(part)


def body(weights_in, speed_modes):
    half = (2, 2, 4, 8, 2, *TILE)
    f32 = jnp.float32
    out = pl.pallas_call(
        kernel,
        out_shape=jax.ShapeDtypeStruct((2, 32, 4, *TILE), f32),
        in_specs=[pl.BlockSpec(memory_space=pltpu.VMEM), pl.BlockSpec(memory_space=pltpu.SMEM)],
        out_specs=pl.BlockSpec(memory_space=pltpu.VMEM),
        scratch_shapes=[
            pltpu.VMEM((2, 32, 32, 128), f32),
            pltpu.VMEM((2, 32, 32, 128), f32),
            pltpu.VMEM((2, *half), f32),
            pltpu.VMEM(half, f32),
            pltpu.VMEM(half, f32),
            pltpu.VMEM((2, 2, 32, 16, 128), f32),
            pltpu.VMEM((2, 32, 32, 128), f32),
            pltpu.VMEM((8, 2, 2, 2, 4, 8, 2, *TILE), f32),
            pltpu.VMEM((2, 2, 4, 8, 2, *TILE), f32),
            pltpu.SemaphoreType.DMA((2, 32)),
            pltpu.SemaphoreType.DMA((2, 32)),
            pltpu.SemaphoreType.DMA((2,)),
            pltpu.SemaphoreType.DMA((2,)),
            pltpu.SemaphoreType.DMA((2, 4, 4)),
            pltpu.SemaphoreType.DMA((2, 4, 4)),
            pltpu.SemaphoreType.DMA((3, 32)),
            pltpu.SemaphoreType.DMA((3, 32)),
        ],
        compiler_params=pltpu.CompilerParams(collective_id=0, has_side_effects=True, vmem_limit_bytes=48 << 20),
    )(weights_in.reshape(2, 32, 4, *TILE), speed_modes)
    return out.reshape(weights_in.shape)


def solution(mesh):
    placed = P(None, None, "sx", "sy", None)
    return jax.shard_map(body, mesh=mesh, in_specs=(placed, P()), out_specs=placed, check_vma=False)
```
